256 devices in a mesh: leaf: 32 (over z, y), front: 8 (over x, core).
Axes of the slice: x: 4, y: 4, z: 8, core: 2. Of those that a mesh axis runs over, the one named last changes fastest.
Arguments:
- leaf_fronts: float32 [32, 1024, 1024], P('leaf', 'front')
- coupling_cols: int32 [32, 8, 124, 128], P('leaf', 'front'), may hold values from 0 to 1023, as said below
- coupling_vals: float32 [32, 8, 124, 128], P('leaf', 'front'), may hold values from -0.1 to 0.1
- sep_diag: float32 [32, 8, 124], P('leaf', 'front'), may hold values from 1 to 3
- child_maps: int32 [62, 512], replicated, may hold values from 0 to 1023, as said below
Outputs:
- factors: float32 [32, 8, 252, 512], P('leaf', 'front')
- log_det: float32 [], replicated
The draws below stay inside these ranges and needn't reach their ends.
Inputs may be any that keep to these rules, and one draw needn't show every extreme that they name: `coupling_cols`: each coupling column is at most the index, in its front, of the row that holds it, so every entry lies on or below the diagonal. `child_maps`: the 512 entries of each row are distinct.
All inputs are finite; a program needn't handle non-finite values.
Results may differ from the reference program's by a relative error of at most 0.0001.
Values sent between devices are 32-bit elements; how exact they have to be, the bound alone decides.
A program may use at most 128 MiB of HBM per device.

```python
import math
import jax
import jax.numpy as jnp
import numpy as np
from jax import lax

SEP = 512
BND = 512
KC = 128
LEVELS = 6
RT = 124
RALL = 252
N_LEAF = 32
N_FRONT = 8


def coupling_rows():
    row_list = []
    for level_no in range(1, LEVELS):
        size_rows = (SEP + BND) // (N_FRONT * 2 ** level_no)
        leaf_ids = np.arange(N_LEAF)[:, None, None]
        front_ids = np.arange(N_FRONT)[None, :, None]
        local_ids = np.arange(size_rows)[None, None, :]
        group_rank = leaf_ids % 2 ** level_no * N_FRONT + front_ids
        row_list.append(np.broadcast_to(group_rank * size_rows + local_ids, (N_LEAF, N_FRONT, size_rows)))
    return np.concatenate(row_list, axis=2).astype(np.int32)


def draw_coupling_cols(key, part):
    upper_ids = jnp.asarray(coupling_rows())[..., None] + 1
    upper_ids = jnp.broadcast_to(upper_ids, (N_LEAF, N_FRONT, RT, KC))
    return jax.random.randint(key, (N_LEAF, N_FRONT, RT, KC), 0, upper_ids, dtype=jnp.int32)


def draw_child_maps(key, part):
    key_list = jax.random.split(jax.random.fold_in(key, 7), 2 * N_LEAF - 2)
    return jax.vmap(lambda one_key: jax.random.permutation(one_key, SEP + BND)[:BND])(key_list).astype(jnp.int32)


def draw_leaf_fronts(key, part):
    width_all = SEP + BND
    key_off, key_diag = jax.random.split(jax.random.fold_in(key, 11))
    shape_all = (N_LEAF, width_all, width_all)
    spread = 0.8 / math.sqrt(width_all)
    entries = jnp.clip(jax.random.normal(key_off, shape_all, jnp.float32), -4.0, 4.0) * spread
    diag_vals = jax.random.uniform(key_diag, (N_LEAF, width_all), jnp.float32, 2.5, 4.0)
    row_grid = lax_iota_rows(width_all)
    identity = row_grid == row_grid.T
    return jnp.where(identity[None], diag_vals[:, :, None], entries)


def lax_iota_rows(width_all):
    return jnp.broadcast_to(jnp.arange(width_all, dtype=jnp.int32)[:, None], (width_all, width_all))


def steps_of(key, dims, cuts, least, top_value):
    factor_of = 1.0
    for axis_at, blocks in cuts:
        draws = jax.random.uniform(jax.random.fold_in(jax.random.fold_in(key, 6), axis_at), (blocks,), jnp.float32, least / len(cuts), top_value / len(cuts))
        factor_of = factor_of * jnp.repeat(jnp.exp(draws), dims[axis_at] // blocks).reshape((-1,) + (1,) * (len(dims) - 1 - axis_at))
    return factor_of


def bell_draw(key, dims, deviation, limit, cuts=(), kind=jnp.bfloat16):
    factor_of = steps_of(key, dims, cuts, -0.22, 0.18) if cuts else 1.0
    values = jax.random.normal(key, dims, jnp.float32) * deviation * factor_of
    return jnp.minimum(jnp.maximum(values, -limit), limit).astype(kind)


def setup_inputs(seed: int = 0) -> dict:
    key_of = jax.random.split(jax.random.key(seed), 6)
    leaf_fronts = draw_leaf_fronts(jax.random.fold_in(key_of[5], 71), 0)
    coupling_cols = draw_coupling_cols(jax.random.fold_in(key_of[5], 71), 0)
    coupling_vals = bell_draw(key_of[2], (N_LEAF, N_FRONT, RT, KC), 0.02, 0.1, ((0, 32), (1, 8)), jnp.float32)
    sep_diag = jnp.clip(jnp.exp(math.log(3.0) - 1.0986123 * jax.random.uniform(key_of[3], (N_LEAF, N_FRONT, RT), jnp.float32) ** steps_of(key_of[3], (N_LEAF, N_FRONT, RT), ((0, 32), (1, 8)), -0.2, 0.2)), 1.0, 3.0)
    child_maps = draw_child_maps(jax.random.fold_in(key_of[5], 71), 0)
    return {"leaf_fronts": leaf_fronts, "coupling_cols": coupling_cols, "coupling_vals": coupling_vals, "sep_diag": sep_diag, "child_maps": child_maps}


highest_precision = lax.Precision.HIGHEST

def symmetric_of(lower_tri):
    return lower_tri + lower_tri.T - jnp.diag(jnp.diag(lower_tri))

def partial_factor(lower_front):
    panel_cols = lower_front[:, :SEP]
    head_block = symmetric_of(panel_cols[:SEP])
    chol_head = jnp.linalg.cholesky(head_block)
    below = jax.scipy.linalg.solve_triangular(chol_head, panel_cols[SEP:].T, lower=True).T
    return (chol_head, below)

def reference(leaf_fronts, coupling_cols, coupling_vals, sep_diag, child_maps):
    width_all = SEP + BND
    factor_out = jnp.zeros((N_LEAF, N_FRONT, RALL, SEP), jnp.float32)
    log_total = jnp.zeros((), jnp.float32)
    updates_now = []
    factor_offset = 0
    list_offset = 0
    map_base = 0
    for level_no in range(LEVELS):
        span_leaf = 2 ** level_no
        size_rows = width_all // (N_FRONT * span_leaf)
        fronts_here = N_LEAF // span_leaf
        updates_next = []
        for front_no in range(fronts_here):
            first_leaf = front_no * span_leaf
            if level_no == 0:
                lower_front = jnp.tril(leaf_fronts[front_no])
            else:
                assembled = jnp.zeros((width_all, width_all), jnp.float32)
                for child_no in range(2):
                    index_map = child_maps[map_base + 2 * front_no + child_no]
                    assembled = assembled.at[index_map[:, None], index_map[None, :]].add(updates_now[2 * front_no + child_no])
                lower_front = jnp.tril(assembled)
                col_block = coupling_cols[first_leaf:first_leaf + span_leaf, :, list_offset:list_offset + size_rows, :].reshape(width_all, KC)
                val_block = coupling_vals[first_leaf:first_leaf + span_leaf, :, list_offset:list_offset + size_rows, :].reshape(width_all, KC)
                row_ids = jnp.arange(width_all, dtype=jnp.int32)
                lower_front = lower_front.at[row_ids[:, None], col_block].add(val_block)
                diag_block = sep_diag[first_leaf:first_leaf + span_leaf, :, list_offset:list_offset + size_rows].reshape(width_all)
                lower_front = lower_front + jnp.diag(diag_block)
            chol_head, below = partial_factor(lower_front)
            log_total = log_total + 2.0 * jnp.sum(jnp.log(jnp.diag(chol_head)))
            factor_cols = jnp.concatenate([chol_head, below], axis=0).reshape(span_leaf, N_FRONT, size_rows, SEP)
            factor_out = factor_out.at[first_leaf:first_leaf + span_leaf, :, factor_offset:factor_offset + size_rows, :].set(factor_cols)
            if level_no < LEVELS - 1:
                product = jnp.dot(below.astype(jnp.float32), below.T.astype(jnp.float32), precision=highest_precision, preferred_element_type=jnp.float32)
                update_low = jnp.tril(lower_front[SEP:, SEP:] - product)
                updates_next.append(symmetric_of(update_low))
        if level_no > 0:
            list_offset = list_offset + size_rows
            map_base = map_base + N_LEAF // 2 ** (level_no - 1)
        factor_offset = factor_offset + size_rows
        updates_now = updates_next
    return (factor_out, log_total)
```

```python
import functools

import jax
import jax.numpy as jnp
from jax import lax
from jax.experimental import pallas as pl
from jax.experimental.pallas import tpu as pltpu
from jax.sharding import PartitionSpec as P

SEP = 512
BND = 512
WIDE = SEP + BND
NB = 128
F32 = jnp.float32
BF16 = jnp.bfloat16
MESH = pl.DeviceIdType.MESH
VMEM_SPEC = pl.BlockSpec(memory_space=pltpu.VMEM)
SMEM_SPEC = pl.BlockSpec(memory_space=pltpu.SMEM)
ANY_SPEC = pl.BlockSpec(memory_space=pl.ANY)
VMEM_LIMIT = 48 * 2**20


def split2(a):
    hi = a.astype(BF16)
    lo = (a - hi.astype(F32)).astype(BF16)
    return hi, lo


def dg(a, b, ca, cb):
    return lax.dot_general(a, b, (((ca,), (cb,)), ((), ())), preferred_element_type=F32)


def dot3(a, b):
    ah, al = split2(a)
    bh, bl = split2(b)
    return dg(ah, bh, 1, 0) + (dg(ah, bl, 1, 0) + dg(al, bh, 1, 0))


def row_of(x, j):
    return jnp.broadcast_to(x[j : j + 1, :], (8, NB))


def col_of(x, k):
    return jnp.broadcast_to(x[:, k : k + 1], (8, NB))


def diag_factor(dref, nref):
    sub = lax.broadcasted_iota(jnp.int32, (8, NB), 0)
    lane = lax.broadcasted_iota(jnp.int32, (8, NB), 1)
    zero = jnp.zeros((8, NB), F32)
    D = [dref[8 * v : 8 * v + 8, :] for v in range(16)]
    N = [jnp.where(lane == sub + 8 * v, 1.0, 0.0) for v in range(16)]
    for b in range(16):
        cols = [col_of(D[b], 8 * b + k) for k in range(8)]
        a = {(i, k): row_of(cols[k], i) for k in range(8) for i in range(k, 8)}
        drow = [row_of(D[b], j) for j in range(8)]
        nrow = [row_of(N[b], j) for j in range(8)]
        r, l, u, n = {}, {}, [], []
        for j in range(8):
            r[j] = lax.rsqrt(a[j, j])
            for i in range(j + 1, 8):
                l[i, j] = a[i, j] * r[j]
            for k in range(j + 1, 8):
                for i in range(k, 8):
                    a[i, k] = a[i, k] - l[i, j] * l[k, j]
            u.append(drow[j] * r[j])
            n.append(nrow[j] * r[j])
            for i in range(j + 1, 8):
                drow[i] = drow[i] - l[i, j] * u[j]
                nrow[i] = nrow[i] - l[i, j] * n[j]
        for v in range(b + 1, 16):
            c = [col_of(D[v], 8 * b + k) for k in range(8)]
            dv, nv = D[v], N[v]
            for j in range(8):
                lj = c[j] * r[j]
                for k in range(j + 1, 8):
                    c[k] = c[k] - lj * l[k, j]
                dv = dv - lj * u[j]
                nv = nv - lj * n[j]
            D[v], N[v] = dv, nv
        db, nb = u[0], n[0]
        for j in range(1, 8):
            db = jnp.where(sub == j, u[j], db)
            nb = jnp.where(sub == j, n[j], nb)
        D[b] = jnp.where(lane >= 8 * b + sub, db, zero)
        N[b] = nb
        dref[8 * b : 8 * b + 8, :] = D[b]
        nref[8 * b : 8 * b + 8, :] = N[b]


def fac_kernel(with_update, size_rows, *refs):
    if with_update:
        pos_ref, t_ref, tail_ref, log_in, piece_ref, log_ref, upd_ref, u_ref, d_ref, n_ref, p_ref = refs
    else:
        pos_ref, t_ref, log_in, piece_ref, log_ref, u_ref, d_ref, n_ref, p_ref = refs
    u_ref[...] = t_ref[...]
    log_ref[...] = log_in[...]
    rows = lax.broadcasted_iota(jnp.int32, (NB, NB), 0)
    cols = lax.broadcasted_iota(jnp.int32, (NB, NB), 1)
    wide = lax.broadcasted_iota(jnp.int32, (NB, WIDE), 1)

    @pl.loop(0, SEP // NB)
    def block(blk):
        o = pl.multiple_of(blk * NB, NB)
        d_ref[...] = u_ref[pl.ds(o, NB), pl.ds(o, NB)]
        diag_factor(d_ref, n_ref)
        d = d_ref[...]
        logs = jnp.where(rows == cols, jnp.log(d), 0.0)
        log_ref[...] += 2.0 * jnp.sum(logs.reshape(16, 8, NB), axis=0)
        strip = dot3(n_ref[...], u_ref[pl.ds(o, NB), :])
        strip = jnp.where(wide >= o + NB, strip, 0.0)
        u_ref[pl.ds(o, NB), :] = strip
        u_ref[pl.ds(o, NB), pl.ds(o, NB)] = d
        sh, sl = split2(strip)

        @pl.loop(blk + 1, SEP // NB)
        def trail(jb):
            q = pl.multiple_of(jb * NB, NB)
            lh, ll = split2(u_ref[pl.ds(o, NB), pl.ds(q, NB)].T)
            u_ref[pl.ds(q, NB), :] -= dg(lh, sh, 1, 0) + (dg(lh, sl, 1, 0) + dg(ll, sh, 1, 0))

    if with_update:
        below = u_ref[:, SEP:]
        bh, bl = split2(below)
        th, tl = split2(below.T)
        upd_ref[...] = tail_ref[...] - (dg(th, bh, 1, 0) + (dg(th, bl, 1, 0) + dg(tl, bh, 1, 0)))
    start = pos_ref[0]
    base = pl.multiple_of(start // NB * NB, NB)
    p_ref[...] = u_ref[:, pl.ds(base, NB)].T
    if size_rows % 8 == 0:
        piece_ref[...] = p_ref[pl.ds(pl.multiple_of(start - base, 8), size_rows), :]
    else:
        part = start % 8
        block8 = p_ref[pl.ds(pl.multiple_of(start - base - part, 8), 8), :]
        picked = block8[:size_rows]
        for first in range(size_rows, 8, size_rows):
            picked = jnp.where(part == first, block8[first : first + size_rows], picked)
        piece_ref[...] = picked


def factor(pos, t, tail, log_acc, size_rows):
    with_update = tail is not None
    outs = [jax.ShapeDtypeStruct((size_rows, SEP), F32), jax.ShapeDtypeStruct((8, NB), F32)]
    if with_update:
        outs.append(jax.ShapeDtypeStruct((BND, BND), F32))
    args = (pos, t, tail, log_acc) if with_update else (pos, t, log_acc)
    return pl.pallas_call(
        functools.partial(fac_kernel, with_update, size_rows),
        out_shape=outs,
        in_specs=[SMEM_SPEC] + [VMEM_SPEC] * (len(args) - 1),
        out_specs=[VMEM_SPEC] * len(outs),
        scratch_shapes=[
            pltpu.VMEM((SEP, WIDE), F32),
            pltpu.VMEM((NB, NB), F32),
            pltpu.VMEM((NB, NB), F32),
            pltpu.VMEM((NB, SEP), F32),
        ],
        compiler_params=pltpu.CompilerParams(vmem_limit_bytes=VMEM_LIMIT),
    )(*args)


def mirrored(square):
    rows = lax.broadcasted_iota(jnp.int32, square.shape, 0)
    cols = lax.broadcasted_iota(jnp.int32, square.shape, 1)
    return jnp.where(rows >= cols, square, square.T)


def asm_kernel(child_count, *refs):
    low_ref = refs[0]
    children = refs[1 : 1 + 2 * child_count]
    t_ref, tail_ref = refs[1 + 2 * child_count :]
    t_sum, tail_sum = None, None
    for child in range(child_count):
        upd_ref, map_ref = children[2 * child : 2 * child + 2]
        ids = lax.broadcasted_iota(jnp.int32, (WIDE, BND), 0)
        pick = jnp.where(ids == map_ref[...], 1.0, 0.0).astype(BF16)
        uh, ul = split2(upd_ref[...])
        xh = dg(pick, uh, 1, 0).astype(BF16)
        xl = dg(pick, ul, 1, 0).astype(BF16)
        t_part = dg(xh[:SEP], pick, 1, 1) + dg(xl[:SEP], pick, 1, 1)
        tail_part = dg(xh[SEP:], pick[SEP:], 1, 1) + dg(xl[SEP:], pick[SEP:], 1, 1)
        if child == 0:
            t_ref[...] = t_part
            tail_ref[...] = tail_part
        else:
            t_ref[...] += t_part
            tail_ref[...] += tail_part
    head = mirrored(low_ref[:SEP, :SEP])
    side = low_ref[SEP:, :SEP].T
    tail = mirrored(low_ref[SEP:, SEP:])
    if child_count:
        t_ref[:, :SEP] += head
        t_ref[:, SEP:] += side
        tail_ref[...] += tail
    else:
        t_ref[:, :SEP] = head
        t_ref[:, SEP:] = side
        tail_ref[...] = tail


def assemble(low, children):
    flat = [part for child in children for part in child]
    return pl.pallas_call(
        functools.partial(asm_kernel, len(children)),
        out_shape=[jax.ShapeDtypeStruct((SEP, WIDE), F32), jax.ShapeDtypeStruct((BND, BND), F32)],
        in_specs=[VMEM_SPEC] * (1 + len(flat)),
        out_specs=[VMEM_SPEC] * 2,
        compiler_params=pltpu.CompilerParams(vmem_limit_bytes=VMEM_LIMIT),
    )(low, *flat)


def couple_kernel(cols_ref, vals_ref, diag_ref, ids_ref, out_ref):
    lane = lax.broadcasted_iota(jnp.int32, (8, NB), 1)

    @pl.loop(0, cols_ref.shape[0] // 8)
    def group(g):
        at = pl.ds(pl.multiple_of(g * 8, 8), 8)
        cols, vals = cols_ref[at, :], vals_ref[at, :]
        row_id = jnp.broadcast_to(ids_ref[at, :], (8, NB))
        diag = jnp.broadcast_to(diag_ref[at, :], (8, NB))
        sums = [jnp.where(row_id == lane + NB * c, diag, 0.0) for c in range(8)]
        for k in range(NB):
            col, val = col_of(cols, k), col_of(vals, k)
            for c in range(8):
                sums[c] = sums[c] + jnp.where(col == lane + NB * c, val, 0.0)
        for c in range(8):
            out_ref[at, NB * c : NB * c + NB] = sums[c]


def couple(cols, vals, diag, ids):
    return pl.pallas_call(
        couple_kernel,
        out_shape=jax.ShapeDtypeStruct((cols.shape[0], WIDE), F32),
        in_specs=[VMEM_SPEC] * 4,
        out_specs=VMEM_SPEC,
        compiler_params=pltpu.CompilerParams(vmem_limit_bytes=VMEM_LIMIT),
    )(cols, vals, diag, ids)


def gather_kernel(count, strip_ref, out_ref, own_sem, send_sem, recv_sem, fsend_sem, frecv_sem):
    me = lax.axis_index("front")
    rows = strip_ref.shape[0]
    chips = count // 2
    chip, core = me // 2, lax.rem(me, 2)
    twin = chip * 2 + 1 - core
    barrier = pltpu.get_barrier_semaphore()
    peers = [lax.rem(chip + d, chips) * 2 + core for d in range(1, chips)]
    for peer in peers + [twin]:
        pl.semaphore_signal(barrier, inc=1, device_id={"front": peer}, device_id_type=MESH)
    pl.semaphore_wait(barrier, chips)

    def at(index):
        return out_ref.at[pl.ds(pl.multiple_of(index * rows, rows), rows), :]

    own = pltpu.make_async_copy(strip_ref, at(me), own_sem)
    own.start()
    first = []
    for d in range(1, chips):
        peer = peers[d - 1]
        copy = pltpu.make_async_remote_copy(
            src_ref=strip_ref, dst_ref=at(me), send_sem=send_sem.at[d - 1], recv_sem=recv_sem.at[d - 1],
            device_id={"front": peer}, device_id_type=MESH,
        )
        copy.start()
        first.append(copy)
    second = []
    for d in range(chips):
        if d == 0:
            src, index = strip_ref, me
        else:
            index = lax.rem(chip - d + chips, chips) * 2 + core
            src = at(index)
            first[d - 1].wait_recv()
        copy = pltpu.make_async_remote_copy(
            src_ref=src, dst_ref=at(index), send_sem=fsend_sem.at[d], recv_sem=frecv_sem.at[d],
            device_id={"front": twin}, device_id_type=MESH,
        )
        copy.start()
        second.append(copy)
    own.wait()
    for copy in second:
        copy.wait_recv()
    for copy in first + second:
        copy.wait_send()


def gather_front(strip, count, cid):
    chips = count // 2
    return pl.pallas_call(
        functools.partial(gather_kernel, count),
        out_shape=jax.ShapeDtypeStruct((count * strip.shape[0], strip.shape[1]), F32),
        in_specs=[VMEM_SPEC],
        out_specs=VMEM_SPEC,
        scratch_shapes=[
            pltpu.SemaphoreType.DMA,
            pltpu.SemaphoreType.DMA((chips,)),
            pltpu.SemaphoreType.DMA((chips,)),
            pltpu.SemaphoreType.DMA((chips,)),
            pltpu.SemaphoreType.DMA((chips,)),
        ],
        compiler_params=pltpu.CompilerParams(
            collective_id=cid, has_side_effects=True, vmem_limit_bytes=VMEM_LIMIT
        ),
    )(strip)


def swap_kernel(count, bit, upd_ref, log_ref, out_ref, log_out, sems, first_sem, send_sem, recv_sem, fsend_sem, frecv_sem):
    leaf = lax.axis_index("leaf")
    me = lax.axis_index("front")
    side = lax.rem(leaf // (1 << bit), 2)
    other = leaf + (1 - 2 * side) * (1 << bit)
    rows = upd_ref.shape[0] // count
    chips = count // 2
    chip, core = me // 2, lax.rem(me, 2)
    twin = chip * 2 + 1 - core
    barrier = pltpu.get_barrier_semaphore()
    peers = [lax.rem(chip + d, chips) * 2 + core for d in range(1, chips)]
    pl.semaphore_signal(barrier, inc=1, device_id={"leaf": other}, device_id_type=MESH)
    for peer in peers + [twin]:
        pl.semaphore_signal(barrier, inc=1, device_id={"front": peer}, device_id_type=MESH)
    pl.semaphore_wait(barrier, chips + 1)

    def at(ref, index):
        return ref.at[pl.ds(pl.multiple_of(index * rows, rows), rows), :]

    cross = pltpu.make_async_remote_copy(
        src_ref=at(upd_ref, me), dst_ref=at(out_ref, me), send_sem=first_sem.at[0], recv_sem=first_sem.at[1],
        device_id={"leaf": other}, device_id_type=MESH,
    )
    cross.start()
    logs = pltpu.make_async_remote_copy(
        src_ref=log_ref, dst_ref=log_out, send_sem=sems.at[0], recv_sem=sems.at[1],
        device_id={"leaf": other}, device_id_type=MESH,
    )
    logs.start()
    cross.wait_recv()
    first = []
    for d in range(1, chips):
        copy = pltpu.make_async_remote_copy(
            src_ref=at(out_ref, me), dst_ref=at(out_ref, me), send_sem=send_sem.at[d - 1], recv_sem=recv_sem.at[d - 1],
            device_id={"front": peers[d - 1]}, device_id_type=MESH,
        )
        copy.start()
        first.append(copy)
    second = []
    for d in range(chips):
        index = lax.rem(chip - d + chips, chips) * 2 + core
        if d:
            first[d - 1].wait_recv()
        copy = pltpu.make_async_remote_copy(
            src_ref=at(out_ref, index), dst_ref=at(out_ref, index), send_sem=fsend_sem.at[d], recv_sem=frecv_sem.at[d],
            device_id={"front": twin}, device_id_type=MESH,
        )
        copy.start()
        second.append(copy)
    logs.wait_recv()
    for copy in second:
        copy.wait_recv()
    for copy in [cross, logs] + first + second:
        copy.wait_send()


def swap_siblings(upd, log_acc, count, bit, cid):
    chips = count // 2
    return pl.pallas_call(
        functools.partial(swap_kernel, count, bit),
        out_shape=[jax.ShapeDtypeStruct(upd.shape, F32), jax.ShapeDtypeStruct(log_acc.shape, F32)],
        in_specs=[VMEM_SPEC] * 2,
        out_specs=[VMEM_SPEC] * 2,
        scratch_shapes=[
            pltpu.SemaphoreType.DMA((2,)),
            pltpu.SemaphoreType.DMA((2,)),
            pltpu.SemaphoreType.DMA((chips,)),
            pltpu.SemaphoreType.DMA((chips,)),
            pltpu.SemaphoreType.DMA((chips,)),
            pltpu.SemaphoreType.DMA((chips,)),
        ],
        compiler_params=pltpu.CompilerParams(
            collective_id=cid, has_side_effects=True, vmem_limit_bytes=VMEM_LIMIT
        ),
    )(upd, log_acc)


def body(leaf_fronts, coupling_cols, coupling_vals, sep_diag, child_maps):
    group_count = lax.axis_size("leaf")
    front_count = lax.axis_size("front")
    level_total = group_count.bit_length()
    leaf_pos = lax.axis_index("leaf")
    front_pos = lax.axis_index("front")
    pieces_out = []

    id_list = []
    for level_no in range(1, level_total):
        size_rows = WIDE // (front_count << level_no)
        rank = (leaf_pos & (1 << level_no) - 1) * front_count + front_pos
        id_list.append(rank * size_rows + jnp.arange(size_rows, dtype=jnp.int32))
    ids = jnp.concatenate(id_list)
    row_total = ids.shape[0]
    pad = -row_total % 8
    cols = jnp.pad(coupling_cols[0, 0], ((0, pad), (0, 0)))
    vals = jnp.pad(coupling_vals[0, 0], ((0, pad), (0, 0)))
    diag = jnp.pad(sep_diag[0, 0], (0, pad))[:, None]
    ids = jnp.pad(ids, (0, pad))[:, None]
    dense = couple(cols, vals, diag, ids)
    lows = []
    offset = 0
    for level_no in range(1, level_total):
        size_rows = WIDE // (front_count << level_no)
        span = 1 << level_no
        strip = dense[offset : offset + size_rows]
        groups = [
            [(g * span + a) * front_count + f for a in range(span) for f in range(front_count)]
            for g in range(group_count // span)
        ]
        lows.append(
            lax.all_gather(strip, ("leaf", "front"), axis=0, tiled=True, axis_index_groups=groups)
            if len(groups) > 1
            else lax.all_gather(strip, ("leaf", "front"), axis=0, tiled=True)
        )
        offset += size_rows

    low = gather_front(leaf_fronts[0], front_count, 0)
    log_acc = jnp.zeros((8, NB), F32)
    t, tail = assemble(low, [])
    map_base = 0
    for level_no in range(level_total):
        span = 1 << level_no
        size_rows = WIDE // (front_count * span)
        rank = (leaf_pos & span - 1) * front_count + front_pos
        pos = jnp.full((1,), rank * size_rows, jnp.int32)
        if level_no + 1 == level_total:
            piece, log_acc = factor(pos, t, None, log_acc, size_rows)
            pieces_out.append(piece)
            break
        piece, log_acc, upd = factor(pos, t, tail, log_acc, size_rows)
        pieces_out.append(piece)
        sib, sib_log = swap_siblings(upd, log_acc, front_count, level_no, 1 + level_no)
        log_acc = log_acc + sib_log
        own_no = leaf_pos >> level_no
        own_map = lax.dynamic_slice_in_dim(child_maps, map_base + own_no, 1, 0)
        sib_map = lax.dynamic_slice_in_dim(child_maps, map_base + (own_no ^ 1), 1, 0)
        t, tail = assemble(lows[level_no], [(upd, own_map), (sib, sib_map)])
        map_base += group_count // span
    log_det = jnp.sum(log_acc)
    factors = jnp.concatenate(pieces_out, axis=0)[None, None]
    return (factors, log_det)


def solution(mesh):
    placed = (
        P("leaf", "front", None),
        P("leaf", "front", None, None),
        P("leaf", "front", None, None),
        P("leaf", "front", None),
        P(),
    )
    return jax.shard_map(
        body,
        mesh=mesh,
        in_specs=placed,
        out_specs=(P("leaf", "front", None, None), P()),
        check_vma=False,
    )
```

```python
import functools

import jax
import jax.numpy as jnp
from jax import lax
from jax.experimental import pallas as pl
from jax.experimental.pallas import tpu as pltpu
from jax.sharding import PartitionSpec as P

SEP = 512
BND = 512
WIDE = SEP + BND
NB = 128
F32 = jnp.float32
BF16 = jnp.bfloat16
MESH = pl.DeviceIdType.MESH
VMEM_SPEC = pl.BlockSpec(memory_space=pltpu.VMEM)
SMEM_SPEC = pl.BlockSpec(memory_space=pltpu.SMEM)
ANY_SPEC = pl.BlockSpec(memory_space=pl.ANY)
VMEM_LIMIT = 28 * 2**20


def split2(a):
    hi = a.astype(BF16)
    lo = (a - hi.astype(F32)).astype(BF16)
    return hi, lo


def dg(a, b, ca, cb):
    return lax.dot_general(a, b, (((ca,), (cb,)), ((), ())), preferred_element_type=F32)


def dot3(a, b):
    ah, al = split2(a)
    bh, bl = split2(b)
    return dg(ah, bh, 1, 0) + (dg(ah, bl, 1, 0) + dg(al, bh, 1, 0))


def row_of(x, j):
    return jnp.broadcast_to(x[j : j + 1, :], (8, NB))


def col_of(x, k):
    return jnp.broadcast_to(x[:, k : k + 1], (8, NB))


def diag_factor(dref, nref):
    sub = lax.broadcasted_iota(jnp.int32, (8, NB), 0)
    lane = lax.broadcasted_iota(jnp.int32, (8, NB), 1)
    zero = jnp.zeros((8, NB), F32)
    D = [dref[8 * v : 8 * v + 8, :] for v in range(16)]
    N = [jnp.where(lane == sub + 8 * v, 1.0, 0.0) for v in range(16)]
    for b in range(16):
        cols = [col_of(D[b], 8 * b + k) for k in range(8)]
        a = {(i, k): row_of(cols[k], i) for k in range(8) for i in range(k, 8)}
        drow = [row_of(D[b], j) for j in range(8)]
        nrow = [row_of(N[b], j) for j in range(8)]
        r, l, u, n = {}, {}, [], []
        for j in range(8):
            r[j] = lax.rsqrt(a[j, j])
            for i in range(j + 1, 8):
                l[i, j] = a[i, j] * r[j]
            for k in range(j + 1, 8):
                for i in range(k, 8):
                    a[i, k] = a[i, k] - l[i, j] * l[k, j]
            u.append(drow[j] * r[j])
            n.append(nrow[j] * r[j])
            for i in range(j + 1, 8):
                drow[i] = drow[i] - l[i, j] * u[j]
                nrow[i] = nrow[i] - l[i, j] * n[j]
        for v in range(b + 1, 16):
            c = [col_of(D[v], 8 * b + k) for k in range(8)]
            dv, nv = D[v], N[v]
            for j in range(8):
                lj = c[j] * r[j]
                for k in range(j + 1, 8):
                    c[k] = c[k] - lj * l[k, j]
                dv = dv - lj * u[j]
                nv = nv - lj * n[j]
            D[v], N[v] = dv, nv
        db, nb = u[0], n[0]
        for j in range(1, 8):
            db = jnp.where(sub == j, u[j], db)
            nb = jnp.where(sub == j, n[j], nb)
        D[b] = jnp.where(lane >= 8 * b + sub, db, zero)
        N[b] = nb
        dref[8 * b : 8 * b + 8, :] = D[b]
        nref[8 * b : 8 * b + 8, :] = N[b]


def fac_kernel(with_update, size_rows, *refs):
    if with_update:
        pos_ref, t_ref, tail_ref, log_in, piece_ref, log_ref, upd_ref, u_ref, d_ref, n_ref, p_ref = refs
    else:
        pos_ref, t_ref, log_in, piece_ref, log_ref, u_ref, d_ref, n_ref, p_ref = refs
    u_ref[...] = t_ref[...]
    log_ref[...] = log_in[...]
    rows = lax.broadcasted_iota(jnp.int32, (NB, NB), 0)
    cols = lax.broadcasted_iota(jnp.int32, (NB, NB), 1)
    wide = lax.broadcasted_iota(jnp.int32, (NB, WIDE), 1)

    @pl.loop(0, SEP // NB)
    def block(blk):
        o = pl.multiple_of(blk * NB, NB)
        d_ref[...] = u_ref[pl.ds(o, NB), pl.ds(o, NB)]
        diag_factor(d_ref, n_ref)
        d = d_ref[...]
        logs = jnp.where(rows == cols, jnp.log(d), 0.0)
        log_ref[...] += 2.0 * jnp.sum(logs.reshape(16, 8, NB), axis=0)
        strip = dot3(n_ref[...], u_ref[pl.ds(o, NB), :])
        strip = jnp.where(wide >= o + NB, strip, 0.0)
        u_ref[pl.ds(o, NB), :] = strip
        u_ref[pl.ds(o, NB), pl.ds(o, NB)] = d
        sh, sl = split2(strip)

        @pl.loop(blk + 1, SEP // NB)
        def trail(jb):
            q = pl.multiple_of(jb * NB, NB)
            lh, ll = split2(u_ref[pl.ds(o, NB), pl.ds(q, NB)].T)
            u_ref[pl.ds(q, NB), :] -= dg(lh, sh, 1, 0) + (dg(lh, sl, 1, 0) + dg(ll, sh, 1, 0))

    if with_update:
        below = u_ref[:, SEP:]
        bh, bl = split2(below)
        th, tl = split2(below.T)
        upd_ref[...] = tail_ref[...] - (dg(th, bh, 1, 0) + (dg(th, bl, 1, 0) + dg(tl, bh, 1, 0)))
    start = pos_ref[0]
    base = pl.multiple_of(start // NB * NB, NB)
    p_ref[...] = u_ref[:, pl.ds(base, NB)].T
    if size_rows % 8 == 0:
        piece_ref[...] = p_ref[pl.ds(pl.multiple_of(start - base, 8), size_rows), :]
    else:
        part = start % 8
        block8 = p_ref[pl.ds(pl.multiple_of(start - base - part, 8), 8), :]
        picked = block8[:size_rows]
        for first in range(size_rows, 8, size_rows):
            picked = jnp.where(part == first, block8[first : first + size_rows], picked)
        piece_ref[...] = picked


def factor(pos, t, tail, log_acc, size_rows):
    with_update = tail is not None
    outs = [jax.ShapeDtypeStruct((size_rows, SEP), F32), jax.ShapeDtypeStruct((8, NB), F32)]
    if with_update:
        outs.append(jax.ShapeDtypeStruct((BND, BND), F32))
    args = (pos, t, tail, log_acc) if with_update else (pos, t, log_acc)
    return pl.pallas_call(
        functools.partial(fac_kernel, with_update, size_rows),
        out_shape=outs,
        in_specs=[SMEM_SPEC] + [VMEM_SPEC] * (len(args) - 1),
        out_specs=[VMEM_SPEC] * len(outs),
        scratch_shapes=[
            pltpu.VMEM((SEP, WIDE), F32),
            pltpu.VMEM((NB, NB), F32),
            pltpu.VMEM((NB, NB), F32),
            pltpu.VMEM((NB, SEP), F32),
        ],
        compiler_params=pltpu.CompilerParams(vmem_limit_bytes=VMEM_LIMIT),
    )(*args)


def mirrored(square):
    rows = lax.broadcasted_iota(jnp.int32, square.shape, 0)
    cols = lax.broadcasted_iota(jnp.int32, square.shape, 1)
    return jnp.where(rows >= cols, square, square.T)


def couple_kernel(cols_ref, vals_ref, diag_ref, ids_ref, out_ref):
    lane = lax.broadcasted_iota(jnp.int32, (8, NB), 1)

    @pl.loop(0, cols_ref.shape[0] // 8)
    def group(g):
        at = pl.ds(pl.multiple_of(g * 8, 8), 8)
        cols, vals = cols_ref[at, :], vals_ref[at, :]
        row_id = jnp.broadcast_to(ids_ref[at, :], (8, NB))
        diag = jnp.broadcast_to(diag_ref[at, :], (8, NB))
        sums = [jnp.where(row_id == lane + NB * c, diag, 0.0) for c in range(8)]
        for k in range(NB):
            col, val = col_of(cols, k), col_of(vals, k)
            for c in range(8):
                sums[c] = sums[c] + jnp.where(col == lane + NB * c, val, 0.0)
        for c in range(8):
            out_ref[at, NB * c : NB * c + NB] = sums[c]


def couple(cols, vals, diag, ids):
    return pl.pallas_call(
        couple_kernel,
        out_shape=jax.ShapeDtypeStruct((cols.shape[0], WIDE), F32),
        in_specs=[VMEM_SPEC] * 4,
        out_specs=VMEM_SPEC,
        compiler_params=pltpu.CompilerParams(vmem_limit_bytes=VMEM_LIMIT),
    )(cols, vals, diag, ids)


def remote(src, dst, send_sem, recv_sem, where):
    return pltpu.make_async_remote_copy(
        src_ref=src, dst_ref=dst, send_sem=send_sem, recv_sem=recv_sem, device_id=where, device_id_type=MESH
    )


def ring_of(count):
    me = lax.axis_index("front")
    chips = count // 2
    chip, core = me // 2, lax.rem(me, 2)
    step = 1 - 2 * core

    def place(offset):
        return lax.rem(chip + offset * step + 2 * chips, chips) * 2 + core

    def twin_of(index):
        return index + 1 - 2 * core

    return me, place, twin_of


def greet(targets):
    barrier = pltpu.get_barrier_semaphore()
    for target in targets:
        pl.semaphore_signal(barrier, inc=1, device_id=target, device_id_type=MESH)
    pl.semaphore_wait(barrier, len(targets))


CUTS = 4
TWIN_SLOT = (1, 0, 2)


def gather_kernel(count, strip_ref, t_ref, tail_ref, land_ref, send_sem, recv_sem):
    me, place, twin_of = ring_of(count)
    rows = strip_ref.shape[0]
    cut = WIDE // CUTS
    ahead, behind, twin = {"front": place(1)}, {"front": place(-1)}, {"front": twin_of(me)}
    greet([ahead, behind, twin])

    def needed(index, c):
        return index * rows // cut >= c

    def move(slot, index, c, where):
        at = land_ref.at[pl.ds(pl.multiple_of(index * rows, rows), rows), cut * c : cut * c + cut]
        src = strip_ref.at[:, cut * c : cut * c + cut] if slot in (0, 1, 3) else at
        return remote(src, at, send_sem.at[slot, c], recv_sem.at[slot, c], where)

    def each(index, act):
        for c in range(CUTS):
            if c == 0:
                act(c)
            else:
                pl.when(needed(index, c))(functools.partial(act, c))

    each(me, lambda c: move(0, me, c, ahead).start())
    each(me, lambda c: move(1, me, c, behind).start())
    each(me, lambda c: move(3, me, c, twin).start())
    land_ref[pl.ds(pl.multiple_of(me * rows, rows), rows), :] = strip_ref[...]
    sources = [place(-1), place(1), place(-2)]

    def arrive(c, k):
        index = sources[k]
        move(k, index, c, ahead).wait_recv()
        if k == 0:
            move(2, index, c, ahead).start()
        move(4 + TWIN_SLOT[k], index, c, twin).start()

    for k in range(3):
        each(sources[k], functools.partial(arrive, k=k))
    for k, index in enumerate([me] + sources):
        each(twin_of(index), lambda c: move(3 + k, twin_of(index), c, twin).wait_recv())
    each(me, lambda c: move(3, me, c, twin).wait_send())
    for k, index in enumerate(sources):
        each(index, lambda c: move(4 + TWIN_SLOT[k], index, c, twin).wait_send())
    each(me, lambda c: move(0, me, c, ahead).wait_send())
    each(me, lambda c: move(1, me, c, behind).wait_send())
    each(sources[0], lambda c: move(2, sources[0], c, ahead).wait_send())
    t_ref[:, :SEP] = mirrored(land_ref[:SEP, :SEP])
    t_ref[:, SEP:] = land_ref[SEP:, :SEP].T
    tail_ref[...] = mirrored(land_ref[SEP:, SEP:])


def gather_front(strip, count, cid):
    return pl.pallas_call(
        functools.partial(gather_kernel, count),
        out_shape=[jax.ShapeDtypeStruct((SEP, WIDE), F32), jax.ShapeDtypeStruct((BND, BND), F32)],
        in_specs=[VMEM_SPEC],
        out_specs=[VMEM_SPEC] * 2,
        scratch_shapes=[
            pltpu.VMEM((WIDE, WIDE), F32),
            pltpu.SemaphoreType.DMA((7, CUTS)),
            pltpu.SemaphoreType.DMA((7, CUTS)),
        ],
        compiler_params=pltpu.CompilerParams(
            collective_id=cid, has_side_effects=True, vmem_limit_bytes=VMEM_LIMIT
        ),
    )(strip)


PART = 32


def chunk_place(index, j):
    first = index // 4 + 1
    if isinstance(index, int):
        return (index, j) if j < first else (15 - index, j - first)
    return jnp.where(j < first, index, 15 - index), jnp.where(j < first, j, j - first)


def pick_of(map_ref):
    ids = lax.broadcasted_iota(jnp.int32, (WIDE, BND), 0)
    return jnp.where(ids == map_ref[...], 1.0, 0.0).astype(BF16)


def swap_kernel(
    count, bit, upd_ref, log_ref, own_map, sib_map, low_ref, t_ref, tail_ref, log_out,
    pack_ref, land_ref, sib_ref, nat_ref, natail_ref, ct_ref, ctail_ref, slog_ref, tlow_ref,
    log_sem, low_sem, send_sem, recv_sem,
):
    leaf = lax.axis_index("leaf")
    side = lax.rem(leaf // (1 << bit), 2)
    other = {"leaf": leaf + (1 - 2 * side) * (1 << bit)}
    me, place, twin_of = ring_of(count)
    ahead, behind, twin = {"front": place(1)}, {"front": place(-1)}, {"front": twin_of(me)}
    for j in range(5):
        rb, cb = chunk_place(me, j)
        pack_ref[PART * j : PART * j + PART, :] = upd_ref[
            pl.ds(pl.multiple_of(rb * PART, PART), PART), pl.ds(pl.multiple_of(cb * NB, NB), NB)
        ]
    greet([other, ahead, behind, twin])

    def move(slot, index, where):
        src = pack_ref if slot == 0 else land_ref.at[index]
        return remote(src, land_ref.at[index], send_sem.at[slot], recv_sem.at[slot], where)

    cross = move(0, me, other)
    cross.start()
    logs = remote(log_ref, slog_ref, log_sem.at[0], log_sem.at[1], other)
    logs.start()

    twin_low = remote(low_ref, tlow_ref, low_sem.at[0], low_sem.at[1], twin)
    twin_low.start()
    pick = pick_of(own_map)
    cross.wait_recv()
    sends = [move(1, me, ahead), move(2, me, behind), move(4, me, twin)]
    for copy in sends:
        copy.start()

    uh, ul = split2(upd_ref[...])
    xh = dg(pick, uh, 1, 0).astype(BF16)
    xl = dg(pick, ul, 1, 0).astype(BF16)
    sources = [place(-1), place(1), place(-2)]
    for k in range(2):
        move(1 + k, sources[k], ahead).wait_recv()
        if k == 0:
            sends.append(move(3, sources[0], ahead))
            sends[-1].start()
        sends.append(move(5 + TWIN_SLOT[k], sources[k], twin))
        sends[-1].start()
    t_ref[...] = dg(xh[:SEP], pick, 1, 1) + dg(xl[:SEP], pick, 1, 1)
    move(3, sources[2], ahead).wait_recv()
    sends.append(move(7, sources[2], twin))
    sends[-1].start()
    tail_ref[...] = dg(xh[SEP:], pick[SEP:], 1, 1) + dg(xl[SEP:], pick[SEP:], 1, 1)
    twin_low.wait_recv()
    span = 2 << bit
    size_rows = WIDE // (count * span)
    core = lax.rem(me, 2)
    for f in range(count):
        for a in range(span):
            src, dst = a * size_rows, (a * count + f) * size_rows
            mine = low_ref[f // 2, src : src + size_rows, :]
            other_rows = tlow_ref[f // 2, src : src + size_rows, :]
            nat_ref[dst : dst + size_rows, :] = jnp.where(core == f % 2, mine, other_rows)
            if dst >= SEP:
                src = SEP // count + src
                mine = low_ref[f // 2, src : src + size_rows, :]
                other_rows = tlow_ref[f // 2, src : src + size_rows, :]
                natail_ref[dst - SEP : dst - SEP + size_rows, :] = jnp.where(core == f % 2, mine, other_rows)
    ct_ref[:, :SEP] = mirrored(nat_ref[:SEP, :])
    ct_ref[:, SEP:] = nat_ref[SEP:, :].T
    ctail_ref[...] = mirrored(natail_ref[...])
    pick = pick_of(sib_map)
    logs.wait_recv()
    log_out[...] = log_ref[...] + slog_ref[...]
    for k, index in enumerate([me] + sources):
        move(4 + k, twin_of(index), twin).wait_recv()
    for copy in [cross, logs, twin_low] + sends:
        copy.wait_send()

    for f in range(count):
        for j in range(5):
            rb, cb = chunk_place(f, j)
            sib_ref[rb * PART : rb * PART + PART, cb * NB : cb * NB + NB] = land_ref[f, PART * j : PART * j + PART, :]
    for rb in range(BND // NB):
        for cb in range(rb):
            sib_ref[cb * NB : cb * NB + NB, rb * NB : rb * NB + NB] = sib_ref[
                rb * NB : rb * NB + NB, cb * NB : cb * NB + NB
            ].T
    uh, ul = split2(sib_ref[...])
    xh = dg(pick, uh, 1, 0).astype(BF16)
    xl = dg(pick, ul, 1, 0).astype(BF16)
    t_ref[...] = (t_ref[...] + (dg(xh[:SEP], pick, 1, 1) + dg(xl[:SEP], pick, 1, 1))) + ct_ref[...]
    tail_ref[...] = (
        tail_ref[...] + (dg(xh[SEP:], pick[SEP:], 1, 1) + dg(xl[SEP:], pick[SEP:], 1, 1))
    ) + ctail_ref[...]


def swap_assemble(upd, log_acc, own_map, sib_map, low, count, bit, cid):
    return pl.pallas_call(
        functools.partial(swap_kernel, count, bit),
        out_shape=[
            jax.ShapeDtypeStruct((SEP, WIDE), F32),
            jax.ShapeDtypeStruct((BND, BND), F32),
            jax.ShapeDtypeStruct((8, NB), F32),
        ],
        in_specs=[VMEM_SPEC] * 5,
        out_specs=[VMEM_SPEC] * 3,
        scratch_shapes=[
            pltpu.VMEM((5 * PART, NB), F32),
            pltpu.VMEM((count, 5 * PART, NB), F32),
            pltpu.VMEM((BND, BND), F32),
            pltpu.VMEM((WIDE, SEP), F32),
            pltpu.VMEM((BND, BND), F32),
            pltpu.VMEM((SEP, WIDE), F32),
            pltpu.VMEM((BND, BND), F32),
            pltpu.VMEM((8, NB), F32),
            pltpu.VMEM((count // 2, 3 * SEP // count, SEP), F32),
            pltpu.SemaphoreType.DMA((2,)),
            pltpu.SemaphoreType.DMA((2,)),
            pltpu.SemaphoreType.DMA((8,)),
            pltpu.SemaphoreType.DMA((8,)),
        ],
        compiler_params=pltpu.CompilerParams(
            collective_id=cid, has_side_effects=True, vmem_limit_bytes=VMEM_LIMIT
        ),
    )(upd, log_acc, own_map, sib_map, low)


def body(leaf_fronts, coupling_cols, coupling_vals, sep_diag, child_maps):
    group_count = lax.axis_size("leaf")
    front_count = lax.axis_size("front")
    level_total = group_count.bit_length()
    leaf_pos = lax.axis_index("leaf")
    front_pos = lax.axis_index("front")
    pieces_out = []

    id_list = []
    for level_no in range(1, level_total):
        size_rows = WIDE // (front_count << level_no)
        rank = (leaf_pos & (1 << level_no) - 1) * front_count + front_pos
        id_list.append(rank * size_rows + jnp.arange(size_rows, dtype=jnp.int32))
    ids = jnp.concatenate(id_list)
    row_total = ids.shape[0]
    pad = -row_total % 8
    cols = jnp.pad(coupling_cols[0, 0], ((0, pad), (0, 0)))
    vals = jnp.pad(coupling_vals[0, 0], ((0, pad), (0, 0)))
    diag = jnp.pad(sep_diag[0, 0], (0, pad))[:, None]
    ids = jnp.pad(ids, (0, pad))[:, None]
    dense = couple(cols, vals, diag, ids)
    near = min(4, group_count)
    far = group_count // near
    y_groups = [[g * near + y for y in range(near)] for g in range(far)]
    z_groups = [[z * near + y for z in range(far)] for y in range(near)]
    y_rows = lax.all_gather(dense, "leaf", axis=0, axis_index_groups=y_groups)
    near_levels = near.bit_length() - 1
    same_core = [list(range(core, front_count, 2)) for core in range(2)]

    def coupling_of(level_no, tie):
        size_rows = WIDE // (front_count << level_no)
        offset = WIDE // front_count - 2 * size_rows
        span = 1 << level_no
        if level_no <= near_levels:
            first = leaf_pos % near // span * span
            strip = lax.dynamic_slice_in_dim(y_rows, first, span, 0)[:, offset : offset + size_rows]
        else:
            deep = span // near
            first = leaf_pos // near // deep * deep
            offset -= deep_offset
            strip = lax.dynamic_slice_in_dim(z_rows, first, deep, 0)[:, :, offset : offset + size_rows]
        strip = strip.reshape(span * size_rows, WIDE)
        strip = jnp.concatenate([strip[:, :SEP], strip[strip.shape[0] // 2 :, SEP:]], axis=0)
        strip, tie = lax.optimization_barrier((strip, tie))
        return lax.all_gather(strip, "front", axis=0, axis_index_groups=same_core), tie

    log_acc = jnp.zeros((8, NB), F32)
    t, tail = gather_front(leaf_fronts[0], front_count, 0)
    map_base = 0
    for level_no in range(level_total):
        span = 1 << level_no
        size_rows = WIDE // (front_count * span)
        rank = (leaf_pos & span - 1) * front_count + front_pos
        pos = jnp.full((1,), rank * size_rows, jnp.int32)
        if level_no == 0 and far > 1:
            deep_offset = WIDE // front_count - 2 * WIDE // (front_count << near_levels + 1)
            y_deep, t = lax.optimization_barrier((y_rows[:, deep_offset:], t))
            z_rows = lax.all_gather(y_deep, "leaf", axis=0, axis_index_groups=z_groups)
        if level_no + 1 < level_total:
            low, t = coupling_of(level_no + 1, t)
        if level_no + 1 == level_total:
            piece, log_acc = factor(pos, t, None, log_acc, size_rows)
            pieces_out.append(piece)
            break
        piece, log_acc, upd = factor(pos, t, tail, log_acc, size_rows)
        pieces_out.append(piece)
        own_no = leaf_pos >> level_no
        own_map = lax.dynamic_slice_in_dim(child_maps, map_base + own_no, 1, 0)
        sib_map = lax.dynamic_slice_in_dim(child_maps, map_base + (own_no ^ 1), 1, 0)
        t, tail, log_acc = swap_assemble(
            upd, log_acc, own_map, sib_map, low, front_count, level_no, 1 + level_no
        )
        map_base += group_count // span
    log_det = jnp.sum(log_acc)
    factors = jnp.concatenate(pieces_out, axis=0)[None, None]
    return (factors, log_det)


def solution(mesh):
    placed = (
        P("leaf", "front", None),
        P("leaf", "front", None, None),
        P("leaf", "front", None, None),
        P("leaf", "front", None),
        P(),
    )
    return jax.shard_map(
        body,
        mesh=mesh,
        in_specs=placed,
        out_specs=(P("leaf", "front", None, None), P()),
        check_vma=False,
    )
```

```python
import functools

import jax
import jax.numpy as jnp
from jax import lax
from jax.experimental import pallas as pl
from jax.experimental.pallas import tpu as pltpu
from jax.sharding import PartitionSpec as P

SEP = 512
BND = 512
WIDE = SEP + BND
NB = 128
F32 = jnp.float32
BF16 = jnp.bfloat16
MESH = pl.DeviceIdType.MESH
VMEM_SPEC = pl.BlockSpec(memory_space=pltpu.VMEM)
SMEM_SPEC = pl.BlockSpec(memory_space=pltpu.SMEM)
HBM_SPEC = pl.BlockSpec(memory_space=pltpu.HBM)
VMEM_LIMIT = 28 * 2**20


def in_hbm(array):
    return pltpu.with_memory_space_constraint(array, pltpu.HBM)


def split2(a):
    hi = a.astype(BF16)
    lo = (a - hi.astype(F32)).astype(BF16)
    return hi, lo


def dg(a, b, ca, cb):
    return lax.dot_general(a, b, (((ca,), (cb,)), ((), ())), preferred_element_type=F32)


def dot3(a, b):
    ah, al = split2(a)
    bh, bl = split2(b)
    return dg(ah, bh, 1, 0) + (dg(ah, bl, 1, 0) + dg(al, bh, 1, 0))


def row_of(x, j):
    return jnp.broadcast_to(x[j : j + 1, :], (8, NB))


def col_of(x, k):
    return jnp.broadcast_to(x[:, k : k + 1], (8, NB))


def diag_factor(dref, nref):
    sub = lax.broadcasted_iota(jnp.int32, (8, NB), 0)
    lane = lax.broadcasted_iota(jnp.int32, (8, NB), 1)
    zero = jnp.zeros((8, NB), F32)
    D = [dref[8 * v : 8 * v + 8, :] for v in range(16)]
    N = [jnp.where(lane == sub + 8 * v, 1.0, 0.0) for v in range(16)]
    for b in range(16):
        cols = [col_of(D[b], 8 * b + k) for k in range(8)]
        a = {(i, k): row_of(cols[k], i) for k in range(8) for i in range(k, 8)}
        drow = [row_of(D[b], j) for j in range(8)]
        nrow = [row_of(N[b], j) for j in range(8)]
        r, l, u, n = {}, {}, [], []
        for j in range(8):
            r[j] = lax.rsqrt(a[j, j])
            for i in range(j + 1, 8):
                l[i, j] = a[i, j] * r[j]
            for k in range(j + 1, 8):
                for i in range(k, 8):
                    a[i, k] = a[i, k] - l[i, j] * l[k, j]
            u.append(drow[j] * r[j])
            n.append(nrow[j] * r[j])
            for i in range(j + 1, 8):
                drow[i] = drow[i] - l[i, j] * u[j]
                nrow[i] = nrow[i] - l[i, j] * n[j]
        for v in range(b + 1, 16):
            c = [col_of(D[v], 8 * b + k) for k in range(8)]
            dv, nv = D[v], N[v]
            for j in range(8):
                lj = c[j] * r[j]
                for k in range(j + 1, 8):
                    c[k] = c[k] - lj * l[k, j]
                dv = dv - lj * u[j]
                nv = nv - lj * n[j]
            D[v], N[v] = dv, nv
        db, nb = u[0], n[0]
        for j in range(1, 8):
            db = jnp.where(sub == j, u[j], db)
            nb = jnp.where(sub == j, n[j], nb)
        D[b] = jnp.where(lane >= 8 * b + sub, db, zero)
        N[b] = nb
        dref[8 * b : 8 * b + 8, :] = D[b]
        nref[8 * b : 8 * b + 8, :] = N[b]


def fac_kernel(level_no, last, offset, size_rows, pos_ref, t_ref, tail_in, *refs):
    if level_no:
        refs = refs[1:]
    out_ref, upd_out, u_ref, d_ref, n_ref, p_ref, piece_ref, tail_ref, upd_ref, sems = refs
    fetch = pltpu.make_async_copy(tail_in, tail_ref, sems.at[0])
    fetch.start()
    u_ref[...] = t_ref[...]
    rows = lax.broadcasted_iota(jnp.int32, (NB, NB), 0)
    cols = lax.broadcasted_iota(jnp.int32, (NB, NB), 1)
    wide = lax.broadcasted_iota(jnp.int32, (NB, WIDE), 1)

    def block(blk, logs):
        o = pl.multiple_of(blk * NB, NB)
        d_ref[...] = u_ref[pl.ds(o, NB), pl.ds(o, NB)]
        diag_factor(d_ref, n_ref)
        d = d_ref[...]
        logs = logs + jnp.sum(jnp.where(rows == cols, jnp.log(d), 0.0).reshape(16, 8, NB), axis=0)
        strip = dot3(n_ref[...], u_ref[pl.ds(o, NB), :])
        strip = jnp.where(wide >= o + NB, strip, 0.0)
        u_ref[pl.ds(o, NB), :] = strip
        u_ref[pl.ds(o, NB), pl.ds(o, NB)] = d
        sh, sl = split2(strip)

        @pl.loop(blk + 1, SEP // NB)
        def trail(jb):
            q = pl.multiple_of(jb * NB, NB)
            lh, ll = split2(u_ref[pl.ds(o, NB), pl.ds(q, NB)].T)
            u_ref[pl.ds(q, NB), :] -= dg(lh, sh, 1, 0) + (dg(lh, sl, 1, 0) + dg(ll, sh, 1, 0))

        return logs

    logs = lax.fori_loop(0, SEP // NB, block, jnp.zeros((8, NB), F32))
    start = pos_ref[level_no]
    base = pl.multiple_of(start // NB * NB, NB)
    p_ref[...] = u_ref[:, pl.ds(base, NB)].T
    if size_rows % 8 == 0:
        piece_ref[...] = p_ref[pl.ds(pl.multiple_of(start - base, 8), size_rows), :]
    else:
        part = start % 8
        block8 = p_ref[pl.ds(pl.multiple_of(start - base - part, 8), 8), :]
        picked = block8[:size_rows]
        for first in range(size_rows, 8, size_rows):
            picked = jnp.where(part == first, block8[first : first + size_rows], picked)
        piece_ref[...] = picked
    store = pltpu.make_async_copy(piece_ref, out_ref.at[offset : offset + size_rows, :], sems.at[1])
    store.start()
    fetch.wait()
    if last:
        upd_out[...] = tail_ref[BND:, :NB] + 2.0 * logs
    else:
        upd_ref[BND:, :NB] = tail_ref[BND:, :NB] + 2.0 * logs
        below = u_ref[:, SEP:]
        bh, bl = split2(below)
        th, tl = split2(below.T)
        moves = []
        for part in range(4):
            at = slice(NB * part, NB * part + NB)
            product = dg(th[at], bh, 1, 0) + (dg(th[at], bl, 1, 0) + dg(tl[at], bh, 1, 0))
            upd_ref[at, :] = tail_ref[at, :] - product
            at = slice(NB * part, NB * part + NB + (8 if part == 3 else 0))
            moves.append(pltpu.make_async_copy(upd_ref.at[at, :], upd_out.at[at, :], sems.at[2 + part]))
            moves[-1].start()
        for move in moves:
            move.wait()
    store.wait()


def factor(level_no, last, offset, size_rows, row_total, pos, t, tail, factors):
    args = [pos, t, in_hbm(tail)] + ([in_hbm(factors)] if level_no else [])
    return pl.pallas_call(
        functools.partial(fac_kernel, level_no, last, offset, size_rows),
        out_shape=[
            pltpu.HBM((row_total, SEP), F32),
            jax.ShapeDtypeStruct((8, NB), F32) if last else pltpu.HBM((BND + 8, BND), F32),
        ],
        in_specs=[SMEM_SPEC, VMEM_SPEC] + [HBM_SPEC] * (len(args) - 2),
        out_specs=[HBM_SPEC, VMEM_SPEC if last else HBM_SPEC],
        scratch_shapes=[
            pltpu.VMEM((SEP, WIDE), F32),
            pltpu.VMEM((NB, NB), F32),
            pltpu.VMEM((NB, NB), F32),
            pltpu.VMEM((NB, SEP), F32),
            pltpu.VMEM((size_rows, SEP), F32),
            pltpu.VMEM((BND + 8, BND), F32),
            pltpu.VMEM((BND + 8, BND), F32),
            pltpu.SemaphoreType.DMA((6,)),
        ],
        input_output_aliases={3: 0} if level_no else {},
        compiler_params=pltpu.CompilerParams(vmem_limit_bytes=VMEM_LIMIT),
    )(*args)


def mirrored(square):
    rows = lax.broadcasted_iota(jnp.int32, square.shape, 0)
    cols = lax.broadcasted_iota(jnp.int32, square.shape, 1)
    return jnp.where(rows >= cols, square, square.T)


def remote(src, dst, send_sem, recv_sem, where):
    return pltpu.make_async_remote_copy(
        src_ref=src, dst_ref=dst, send_sem=send_sem, recv_sem=recv_sem, device_id=where, device_id_type=MESH
    )


def ring_of(count):
    me = lax.axis_index("front")
    chips = count // 2
    chip, core = me // 2, lax.rem(me, 2)
    step = 1 - 2 * core

    def place(offset):
        return lax.rem(chip + offset * step + 2 * chips, chips) * 2 + core

    def twin_of(index):
        return index + 1 - 2 * core

    return me, place, twin_of


def greet(targets):
    barrier = pltpu.get_barrier_semaphore()
    for target in targets:
        pl.semaphore_signal(barrier, inc=1, device_id=target, device_id_type=MESH)
    pl.semaphore_wait(barrier, len(targets))


CUTS = 4
TWIN_SLOT = (1, 0, 2)


def coupling_rows(me, leaf, count, levels, cols_ref, vals_ref, diag_ref, dense_ref, deep_ref):
    sub = lax.broadcasted_iota(jnp.int32, (8, WIDE), 0)
    lane = lax.broadcasted_iota(jnp.int32, (8, WIDE), 1)

    def expand(cols, vals, diag, first_id):
        sums = jnp.where(lane == sub + first_id, jnp.broadcast_to(diag, (8, WIDE)), 0.0)
        for k in range(NB):
            col = jnp.broadcast_to(cols[:, k : k + 1], (8, WIDE))
            val = jnp.broadcast_to(vals[:, k : k + 1], (8, WIDE))
            sums = sums + jnp.where(col == lane, val, 0.0)
        return sums

    def first_row(level_no, local):
        size_rows = WIDE // (count << level_no)
        return (lax.rem(leaf, 1 << level_no) * count + me) * size_rows + local

    rows = cols_ref.shape[0]

    @pl.loop(0, rows // 8)
    def group(g):
        at = pl.ds(pl.multiple_of(g * 8, 8), 8)
        first_id = first_row(1, g * 8)
        for level_no in range(2, levels):
            begin = WIDE // count - 2 * (WIDE // (count << level_no))
            first_id = jnp.where(g * 8 >= begin, first_row(level_no, g * 8 - begin), first_id)
        dense_ref[at, :] = expand(cols_ref[at, :], vals_ref[at, :], diag_ref[at, :], first_id)

    odd = rows % 8
    if odd:
        def tail_of(ref):
            part = ref[rows - odd : rows, :]
            return jnp.concatenate([part] * (8 // odd), axis=0)

        sums = expand(tail_of(cols_ref), tail_of(vals_ref), tail_of(diag_ref), first_row(levels - 1, 0))
        deep_ref[...] = jnp.concatenate([sums[:odd, :SEP], sums[:odd, SEP:]], axis=0)


def level_rows(count, level_no):
    size_rows = WIDE // (count << level_no)
    return size_rows, WIDE // count - 2 * size_rows


def leaf_copies(leaf, count, level_no, dense_ref, deep_ref, pack_ref, deep_land, sems, sending, act):
    span = 1 << level_no
    size_rows, begin = level_rows(count, level_no)
    own = lax.rem(leaf, span)

    @pl.loop(1, span)
    def step(d):
        a = own if sending else lax.rem(own - d + span, span)
        where = {"leaf": leaf - own + (lax.rem(own + d, span) if sending else own)}
        if size_rows % 8:
            act(remote(deep_ref, deep_land.at[a], sems.at[0, 0, d], sems.at[1, 0, d], where))
            return
        left = pl.ds(pl.multiple_of(a * size_rows, size_rows), size_rows)
        src = dense_ref.at[begin : begin + size_rows, :SEP]
        act(remote(src, pack_ref.at[left, :], sems.at[0, 0, d], sems.at[1, 0, d], where))

        @pl.when(a >= span // 2)
        def right_part():
            right = pl.ds(pl.multiple_of(a * size_rows + SEP // count, size_rows), size_rows)
            src = dense_ref.at[begin : begin + size_rows, SEP:]
            act(remote(src, pack_ref.at[right, :], sems.at[0, 1, d], sems.at[1, 1, d], where))


def own_copies(leaf, count, level_no, dense_ref, deep_ref, pack_ref, deep_land, sems, act):
    span = 1 << level_no
    size_rows, begin = level_rows(count, level_no)
    own = lax.rem(leaf, span)
    if size_rows % 8:
        act(pltpu.make_async_copy(deep_ref, deep_land.at[own], sems.at[0, 0, 0]))
        return
    left = pl.ds(pl.multiple_of(own * size_rows, size_rows), size_rows)
    act(pltpu.make_async_copy(dense_ref.at[begin : begin + size_rows, :SEP], pack_ref.at[left, :], sems.at[0, 0, 0]))

    @pl.when(own >= span // 2)
    def right_part():
        right = pl.ds(pl.multiple_of(own * size_rows + SEP // count, size_rows), size_rows)
        src = dense_ref.at[begin : begin + size_rows, SEP:]
        act(pltpu.make_async_copy(src, pack_ref.at[right, :], sems.at[0, 1, 0]))


def start(copy):
    copy.start()


def gather_kernel(
    count, levels, strip_ref, cols_ref, vals_ref, diag_ref, t_ref, tail_out, pack_ref, dense_out, deep_out,
    land_ref, dense_ref, deep_ref, tail_ref, send_sem, recv_sem, leaf_sem, out_sem,
):
    leaf = lax.axis_index("leaf")
    me, place, twin_of = ring_of(count)
    rows = strip_ref.shape[0]
    cut = WIDE // CUTS
    ahead, behind, twin = {"front": place(1)}, {"front": place(-1)}, {"front": twin_of(me)}
    greet([ahead, behind, twin, {"leaf": leaf + 1 - 2 * lax.rem(leaf, 2)}])

    def needed(index, c):
        return index * rows // cut >= c

    def move(slot, index, c, where):
        at = land_ref.at[pl.ds(pl.multiple_of(index * rows, rows), rows), cut * c : cut * c + cut]
        src = strip_ref.at[:, cut * c : cut * c + cut] if slot in (0, 1, 3) else at
        return remote(src, at, send_sem.at[slot, c], recv_sem.at[slot, c], where)

    def each(index, act):
        for c in range(CUTS):
            if c == 0:
                act(c)
            else:
                pl.when(needed(index, c))(functools.partial(act, c))

    each(me, lambda c: move(0, me, c, ahead).start())
    each(me, lambda c: move(1, me, c, behind).start())
    each(me, lambda c: move(3, me, c, twin).start())
    land_ref[pl.ds(pl.multiple_of(me * rows, rows), rows), :] = strip_ref[...]
    coupling_rows(me, leaf, count, levels, cols_ref, vals_ref, diag_ref, dense_ref, deep_ref)
    parts = (leaf, count, 1, dense_ref, deep_ref, pack_ref, None, leaf_sem)
    leaf_copies(*parts, True, start)
    own_copies(*parts, start)
    outs = [
        pltpu.make_async_copy(dense_ref, dense_out, out_sem.at[0]),
        pltpu.make_async_copy(deep_ref, deep_out, out_sem.at[1]),
    ]
    for copy in outs:
        copy.start()
    sources = [place(-1), place(1), place(-2)]

    def arrive(c, k):
        index = sources[k]
        move(k, index, c, ahead).wait_recv()
        if k == 0:
            move(2, index, c, ahead).start()
        move(4 + TWIN_SLOT[k], index, c, twin).start()

    for k in range(3):
        each(sources[k], functools.partial(arrive, k=k))
    for k, index in enumerate([me] + sources):
        each(twin_of(index), lambda c: move(3 + k, twin_of(index), c, twin).wait_recv())
    tail_ref[:BND, :] = mirrored(land_ref[SEP:, SEP:])
    tail_ref[BND:, :] = jnp.zeros((8, BND), F32)
    outs.append(pltpu.make_async_copy(tail_ref, tail_out, out_sem.at[2]))
    outs[-1].start()
    t_ref[:, :SEP] = mirrored(land_ref[:SEP, :SEP])
    t_ref[:, SEP:] = land_ref[SEP:, :SEP].T
    each(me, lambda c: move(3, me, c, twin).wait_send())
    for k, index in enumerate(sources):
        each(index, lambda c: move(4 + TWIN_SLOT[k], index, c, twin).wait_send())
    each(me, lambda c: move(0, me, c, ahead).wait_send())
    each(me, lambda c: move(1, me, c, behind).wait_send())
    each(sources[0], lambda c: move(2, sources[0], c, ahead).wait_send())
    leaf_copies(*parts, False, lambda copy: copy.wait_recv())
    leaf_copies(*parts, True, lambda copy: copy.wait_send())
    own_copies(*parts, lambda copy: copy.wait())
    for copy in outs:
        copy.wait()


def gather_front(strip, cols, vals, diag, count, leaves, cid):
    levels = leaves.bit_length()
    return pl.pallas_call(
        functools.partial(gather_kernel, count, levels),
        out_shape=[
            jax.ShapeDtypeStruct((SEP, WIDE), F32),
            pltpu.HBM((BND + 8, BND), F32),
            pltpu.HBM((3 * SEP // count, SEP), F32),
            pltpu.HBM((WIDE // count, WIDE), F32),
            pltpu.HBM((8, SEP), F32),
        ],
        in_specs=[VMEM_SPEC] * 4,
        out_specs=[VMEM_SPEC] + [HBM_SPEC] * 4,
        scratch_shapes=[
            pltpu.VMEM((WIDE, WIDE), F32),
            pltpu.VMEM((WIDE // count, WIDE), F32),
            pltpu.VMEM((8, SEP), F32),
            pltpu.VMEM((BND + 8, BND), F32),
            pltpu.SemaphoreType.DMA((7, CUTS)),
            pltpu.SemaphoreType.DMA((7, CUTS)),
            pltpu.SemaphoreType.DMA((2, 2, 2)),
            pltpu.SemaphoreType.DMA((3,)),
        ],
        compiler_params=pltpu.CompilerParams(
            collective_id=cid, has_side_effects=True, vmem_limit_bytes=VMEM_LIMIT
        ),
    )(strip, cols, vals, diag)


PART = 32


def chunk_place(index, j):
    first = index // 4 + 1
    if isinstance(index, int):
        return (index, j) if j < first else (15 - index, j - first)
    return jnp.where(j < first, index, 15 - index), jnp.where(j < first, j, j - first)


def pick_of(maps_ref, row):
    ids = lax.broadcasted_iota(jnp.int32, (WIDE, BND), 0)
    return jnp.where(ids == maps_ref[pl.ds(row, 1), :], 1.0, 0.0).astype(BF16)


def swap_kernel(count, bit, map_base, hosts, upd_in, maps_ref, low_in, *refs):
    dense_ref = deep_ref = pack_out = deep_land = None
    if hosts:
        dense_ref, deep_ref, t_ref, tail_out, pack_out, *refs = refs
    else:
        t_ref, tail_out, *refs = refs
    (
        pack_ref, land_ref, sib_ref, nat_ref, natail_ref, ct_ref, ctail_ref, slog_ref, low_ref, tlow_ref,
        upd_ref, tail_ref, log_sem, low_sem, send_sem, recv_sem, *refs,
    ) = refs
    host_level = bit + 2
    span = 1 << host_level if hosts else 2
    odd = hosts and level_rows(count, host_level)[0] % 8 != 0
    fetch = pltpu.make_async_copy(upd_in, upd_ref, low_sem.at[3])
    fetch.start()
    leaf = lax.axis_index("leaf")
    side = lax.rem(leaf // (1 << bit), 2)
    other = {"leaf": leaf + (1 - 2 * side) * (1 << bit)}
    me, place, twin_of = ring_of(count)
    ahead, behind, twin = {"front": place(1)}, {"front": place(-1)}, {"front": twin_of(me)}
    barrier = pltpu.get_barrier_semaphore()
    for target in [ahead, behind, twin] + ([] if hosts else [other]):
        pl.semaphore_signal(barrier, inc=1, device_id=target, device_id_type=MESH)
    if hosts:
        @pl.loop(1, span)
        def greet_leaf(d):
            own = lax.rem(leaf, span)
            where = {"leaf": leaf - own + lax.rem(own + d, span)}
            pl.semaphore_signal(barrier, inc=1, device_id=where, device_id_type=MESH)

        host_sem = refs[0]
        if odd:
            deep_land, gathered_ref = refs[1:]
        parts = (leaf, count, host_level, dense_ref, deep_ref, pack_out, deep_land, host_sem)
        own_copies(*parts, start)
    fetch.wait()
    for j in range(5):
        rb, cb = chunk_place(me, j)
        pack_ref[PART * j : PART * j + PART, :] = upd_ref[
            pl.ds(pl.multiple_of(rb * PART, PART), PART), pl.ds(pl.multiple_of(cb * NB, NB), NB)
        ]
    pl.semaphore_wait(barrier, 3 + span - 1)

    def move(slot, index, where):
        src = pack_ref if slot == 0 else land_ref.at[index]
        return remote(src, land_ref.at[index], send_sem.at[slot], recv_sem.at[slot], where)

    cross = move(0, me, other)
    cross.start()
    logs = remote(upd_ref.at[BND:, :NB], slog_ref, log_sem.at[0], log_sem.at[1], other)
    logs.start()

    twin_low = remote(low_in, tlow_ref, low_sem.at[0], low_sem.at[1], twin)
    twin_low.start()
    own_low = pltpu.make_async_copy(low_in, low_ref, low_sem.at[2])
    own_low.start()
    if hosts:
        leaf_copies(*parts, True, start)
    own_row = map_base + leaf // (1 << bit)
    pick = pick_of(maps_ref, own_row)
    cross.wait_recv()
    sends = [move(1, me, ahead), move(2, me, behind), move(4, me, twin)]
    for copy in sends:
        copy.start()

    uh, ul = split2(upd_ref[:BND, :])
    xh = dg(pick, uh, 1, 0).astype(BF16)
    xl = dg(pick, ul, 1, 0).astype(BF16)
    sources = [place(-1), place(1), place(-2)]
    for k in range(2):
        move(1 + k, sources[k], ahead).wait_recv()
        if k == 0:
            sends.append(move(3, sources[0], ahead))
            sends[-1].start()
        sends.append(move(5 + TWIN_SLOT[k], sources[k], twin))
        sends[-1].start()
    t_ref[...] = dg(xh[:SEP], pick, 1, 1) + dg(xl[:SEP], pick, 1, 1)
    move(3, sources[2], ahead).wait_recv()
    sends.append(move(7, sources[2], twin))
    sends[-1].start()
    tail_ref[:BND, :] = dg(xh[SEP:], pick[SEP:], 1, 1) + dg(xl[SEP:], pick[SEP:], 1, 1)
    own_low.wait()
    twin_low.wait_recv()
    size_rows = WIDE // (count << bit + 1)
    core = lax.rem(me, 2)
    for f in range(count):
        for a in range(2 << bit):
            src, dst = a * size_rows, (a * count + f) * size_rows
            mine = low_ref[f // 2, src : src + size_rows, :]
            other_rows = tlow_ref[f // 2, src : src + size_rows, :]
            nat_ref[dst : dst + size_rows, :] = jnp.where(core == f % 2, mine, other_rows)
            if dst >= SEP:
                src = SEP // count + src
                mine = low_ref[f // 2, src : src + size_rows, :]
                other_rows = tlow_ref[f // 2, src : src + size_rows, :]
                natail_ref[dst - SEP : dst - SEP + size_rows, :] = jnp.where(core == f % 2, mine, other_rows)
    ct_ref[:, :SEP] = mirrored(nat_ref[:SEP, :])
    ct_ref[:, SEP:] = nat_ref[SEP:, :].T
    ctail_ref[...] = mirrored(natail_ref[...])
    pick = pick_of(maps_ref, own_row + 1 - 2 * side)
    logs.wait_recv()
    tail_ref[BND:, :NB] = upd_ref[BND:, :NB] + slog_ref[...]
    for k, index in enumerate([me] + sources):
        move(4 + k, twin_of(index), twin).wait_recv()
    for copy in [cross, logs, twin_low] + sends:
        copy.wait_send()

    for f in range(count):
        for j in range(5):
            rb, cb = chunk_place(f, j)
            sib_ref[rb * PART : rb * PART + PART, cb * NB : cb * NB + NB] = land_ref[f, PART * j : PART * j + PART, :]
    for rb in range(BND // NB):
        for cb in range(rb):
            sib_ref[cb * NB : cb * NB + NB, rb * NB : rb * NB + NB] = sib_ref[
                rb * NB : rb * NB + NB, cb * NB : cb * NB + NB
            ].T
    uh, ul = split2(sib_ref[...])
    xh = dg(pick, uh, 1, 0).astype(BF16)
    xl = dg(pick, ul, 1, 0).astype(BF16)
    tail_ref[:BND, :] = (
        tail_ref[:BND, :] + (dg(xh[SEP:], pick[SEP:], 1, 1) + dg(xl[SEP:], pick[SEP:], 1, 1))
    ) + ctail_ref[...]
    tail_move = pltpu.make_async_copy(tail_ref, tail_out, low_sem.at[4])
    tail_move.start()
    t_ref[...] = (t_ref[...] + (dg(xh[:SEP], pick, 1, 1) + dg(xl[:SEP], pick, 1, 1))) + ct_ref[...]
    if hosts:
        leaf_copies(*parts, False, lambda copy: copy.wait_recv())
        own_copies(*parts, lambda copy: copy.wait())
        if odd:
            size_rows, _ = level_rows(count, host_level)
            for a in range(span):
                gathered_ref[a * size_rows : (a + 1) * size_rows, :] = deep_land[a, :size_rows, :]
                if a >= span // 2:
                    first = SEP // count + a * size_rows
                    gathered_ref[first : first + size_rows, :] = deep_land[a, size_rows : 2 * size_rows, :]
            pack_move = pltpu.make_async_copy(gathered_ref, pack_out, low_sem.at[5])
            pack_move.start()
            pack_move.wait()
        leaf_copies(*parts, True, lambda copy: copy.wait_send())
    tail_move.wait()


def swap_assemble(upd, maps, low, dense, deep, count, bit, map_base, levels, cid):
    hosts = bit + 2 < levels
    args = [in_hbm(upd), maps, in_hbm(low)] + ([in_hbm(dense), in_hbm(deep)] if hosts else [])
    pack_shape = (3 * SEP // count, SEP)
    outs = [jax.ShapeDtypeStruct((SEP, WIDE), F32), pltpu.HBM((BND + 8, BND), F32)]
    scratch = [
        pltpu.VMEM((5 * PART, NB), F32),
        pltpu.VMEM((count, 5 * PART, NB), F32),
        pltpu.VMEM((BND, BND), F32),
        pltpu.VMEM((WIDE, SEP), F32),
        pltpu.VMEM((BND, BND), F32),
        pltpu.VMEM((SEP, WIDE), F32),
        pltpu.VMEM((BND, BND), F32),
        pltpu.VMEM((8, NB), F32),
        pltpu.VMEM((count // 2,) + pack_shape, F32),
        pltpu.VMEM((count // 2,) + pack_shape, F32),
        pltpu.VMEM((BND + 8, BND), F32),
        pltpu.VMEM((BND + 8, BND), F32),
        pltpu.SemaphoreType.DMA((2,)),
        pltpu.SemaphoreType.DMA((6,)),
        pltpu.SemaphoreType.DMA((8,)),
        pltpu.SemaphoreType.DMA((8,)),
    ]
    if hosts:
        span = 4 << bit
        scratch.append(pltpu.SemaphoreType.DMA((2, 2, span)))
        if level_rows(count, bit + 2)[0] % 8:
            scratch += [pltpu.VMEM((span, 8, SEP), F32), pltpu.VMEM(pack_shape, F32)]
    return pl.pallas_call(
        functools.partial(swap_kernel, count, bit, map_base, hosts),
        out_shape=outs + ([pltpu.HBM(pack_shape, F32)] if hosts else []),
        in_specs=[HBM_SPEC, VMEM_SPEC, HBM_SPEC] + [HBM_SPEC] * (len(args) - 3),
        out_specs=[VMEM_SPEC, HBM_SPEC] + [HBM_SPEC] * hosts,
        scratch_shapes=scratch,
        compiler_params=pltpu.CompilerParams(
            collective_id=cid, has_side_effects=True, vmem_limit_bytes=VMEM_LIMIT
        ),
    )(*args)


def body(leaf_fronts, coupling_cols, coupling_vals, sep_diag, child_maps):
    group_count = lax.axis_size("leaf")
    front_count = lax.axis_size("front")
    level_total = group_count.bit_length()
    leaf_pos = lax.axis_index("leaf")
    front_pos = lax.axis_index("front")
    sizes = [WIDE // (front_count << level_no) for level_no in range(level_total)]
    pos = jnp.stack(
        [((leaf_pos & (1 << n) - 1) * front_count + front_pos) * sizes[n] for n in range(level_total)]
    ).astype(jnp.int32)
    same_core = [list(range(core, front_count, 2)) for core in range(2)]
    t, tail, pack, dense, deep = gather_front(
        leaf_fronts[0], coupling_cols[0, 0], coupling_vals[0, 0], sep_diag[0, 0][:, None], front_count, group_count, 0
    )
    factors = None
    map_base = 0
    offset = 0
    for level_no in range(level_total):
        last = level_no + 1 == level_total
        if not last:
            low = lax.all_gather(pack, "front", axis=0, axis_index_groups=same_core)
        factors, upd = factor(level_no, last, offset, sizes[level_no], sum(sizes), pos, t, tail, factors)
        offset += sizes[level_no]
        if last:
            break
        t, tail, *pack = swap_assemble(
            upd, child_maps, low, dense, deep, front_count, level_no, map_base, level_total, 1 + level_no
        )
        pack = pack[0] if pack else None
        map_base += group_count >> level_no
    return (factors[None, None], jnp.sum(upd))


def solution(mesh):
    placed = (
        P("leaf", "front", None),
        P("leaf", "front", None, None),
        P("leaf", "front", None, None),
        P("leaf", "front", None),
        P(),
    )
    return jax.shard_map(
        body,
        mesh=mesh,
        in_specs=placed,
        out_specs=(P("leaf", "front", None, None), P()),
        check_vma=False,
    )
```

```python
import functools

import jax
import jax.numpy as jnp
from jax import lax
from jax.experimental import pallas as pl
from jax.experimental.pallas import tpu as pltpu
from jax.sharding import PartitionSpec as P

SEP = 512
BND = 512
WIDE = SEP + BND
NB = 128
F32 = jnp.float32
BF16 = jnp.bfloat16
MESH = pl.DeviceIdType.MESH
VMEM_SPEC = pl.BlockSpec(memory_space=pltpu.VMEM)
SMEM_SPEC = pl.BlockSpec(memory_space=pltpu.SMEM)
HBM_SPEC = pl.BlockSpec(memory_space=pltpu.HBM)
VMEM_LIMIT = 28 * 2**20


def in_hbm(array):
    return pltpu.with_memory_space_constraint(array, pltpu.HBM)


def split2(a):
    hi = a.astype(BF16)
    lo = (a - hi.astype(F32)).astype(BF16)
    return hi, lo


def dg(a, b, ca, cb):
    return lax.dot_general(a, b, (((ca,), (cb,)), ((), ())), preferred_element_type=F32)


def dot3(a, b):
    ah, al = split2(a)
    bh, bl = split2(b)
    return dg(ah, bh, 1, 0) + (dg(ah, bl, 1, 0) + dg(al, bh, 1, 0))


def row_of(x, j):
    return jnp.broadcast_to(x[j : j + 1, :], (8, NB))


def col_of(x, k):
    return jnp.broadcast_to(x[:, k : k + 1], (8, NB))


def diag_factor(dref, nref):
    sub = lax.broadcasted_iota(jnp.int32, (8, NB), 0)
    lane = lax.broadcasted_iota(jnp.int32, (8, NB), 1)
    zero = jnp.zeros((8, NB), F32)
    D = [dref[8 * v : 8 * v + 8, :] for v in range(16)]
    N = [jnp.where(lane == sub + 8 * v, 1.0, 0.0) for v in range(16)]
    for b in range(16):
        cols = ahead if b else [col_of(D[0], k) for k in range(8)]
        if b < 15:
            ahead = [col_of(D[b + 1], 8 * b + 8 + k) for k in range(8)]
        a = {(i, k): row_of(cols[k], i) for k in range(8) for i in range(k, 8)}
        drow = [row_of(D[b], j) for j in range(8)]
        nrow = [row_of(N[b], j) for j in range(8)]
        r, l, u, n = {}, {}, [], []
        for j in range(8):
            r[j] = lax.rsqrt(a[j, j])
            for i in range(j + 1, 8):
                l[i, j] = a[i, j] * r[j]
            for k in range(j + 1, 8):
                for i in range(k, 8):
                    a[i, k] = a[i, k] - l[i, j] * l[k, j]
            u.append(drow[j] * r[j])
            n.append(nrow[j] * r[j])
            for i in range(j + 1, 8):
                drow[i] = drow[i] - l[i, j] * u[j]
                nrow[i] = nrow[i] - l[i, j] * n[j]
        for v in range(b + 1, 16):
            c = [col_of(D[v], 8 * b + k) for k in range(8)]
            dv, nv = D[v], N[v]
            for j in range(8):
                lj = c[j] * r[j]
                for k in range(j + 1, 8):
                    c[k] = c[k] - lj * l[k, j]
                if v == b + 1:
                    ahead = [ahead[k] - lj * row_of(lj, k) for k in range(8)]
                dv = dv - lj * u[j]
                nv = nv - lj * n[j]
            D[v], N[v] = dv, nv
        db, nb = u[0], n[0]
        for j in range(1, 8):
            db = jnp.where(sub == j, u[j], db)
            nb = jnp.where(sub == j, n[j], nb)
        D[b] = jnp.where(lane >= 8 * b + sub, db, zero)
        N[b] = nb
        dref[8 * b : 8 * b + 8, :] = D[b]
        nref[8 * b : 8 * b + 8, :] = N[b]


def fac_kernel(level_no, last, offset, size_rows, pos_ref, t_ref, tail_in, *refs):
    if level_no:
        refs = refs[1:]
    out_ref, upd_out, u_ref, d_ref, n_ref, p_ref, piece_ref, tail_ref, upd_ref, sems = refs
    fetch = pltpu.make_async_copy(tail_in, tail_ref, sems.at[0])
    fetch.start()
    u_ref[...] = t_ref[...]
    rows = lax.broadcasted_iota(jnp.int32, (NB, NB), 0)
    cols = lax.broadcasted_iota(jnp.int32, (NB, NB), 1)
    wide = lax.broadcasted_iota(jnp.int32, (NB, WIDE), 1)

    def block(blk, logs):
        o = pl.multiple_of(blk * NB, NB)
        d_ref[...] = u_ref[pl.ds(o, NB), pl.ds(o, NB)]
        diag_factor(d_ref, n_ref)
        d = d_ref[...]
        logs = logs + jnp.sum(jnp.where(rows == cols, jnp.log(d), 0.0).reshape(16, 8, NB), axis=0)
        strip = dot3(n_ref[...], u_ref[pl.ds(o, NB), :])
        strip = jnp.where(wide >= o + NB, strip, 0.0)
        u_ref[pl.ds(o, NB), :] = strip
        u_ref[pl.ds(o, NB), pl.ds(o, NB)] = d
        sh, sl = split2(strip)

        @pl.loop(blk + 1, SEP // NB)
        def trail(jb):
            q = pl.multiple_of(jb * NB, NB)
            lh, ll = split2(u_ref[pl.ds(o, NB), pl.ds(q, NB)].T)
            u_ref[pl.ds(q, NB), :] -= dg(lh, sh, 1, 0) + (dg(lh, sl, 1, 0) + dg(ll, sh, 1, 0))

        return logs

    logs = lax.fori_loop(0, SEP // NB, block, jnp.zeros((8, NB), F32))
    start = pos_ref[level_no]
    base = pl.multiple_of(start // NB * NB, NB)
    p_ref[...] = u_ref[:, pl.ds(base, NB)].T
    if size_rows % 8 == 0:
        piece_ref[...] = p_ref[pl.ds(pl.multiple_of(start - base, 8), size_rows), :]
    else:
        part = start % 8
        block8 = p_ref[pl.ds(pl.multiple_of(start - base - part, 8), 8), :]
        picked = block8[:size_rows]
        for first in range(size_rows, 8, size_rows):
            picked = jnp.where(part == first, block8[first : first + size_rows], picked)
        piece_ref[...] = picked
    store = pltpu.make_async_copy(piece_ref, out_ref.at[offset : offset + size_rows, :], sems.at[1])
    store.start()
    fetch.wait()
    if last:
        upd_out[...] = tail_ref[BND:, :NB] + 2.0 * logs
    else:
        upd_ref[BND:, :NB] = tail_ref[BND:, :NB] + 2.0 * logs
        below = u_ref[:, SEP:]
        bh, bl = split2(below)
        th, tl = split2(below.T)
        moves = []
        for part in range(4):
            at = slice(NB * part, NB * part + NB)
            product = dg(th[at], bh, 1, 0) + (dg(th[at], bl, 1, 0) + dg(tl[at], bh, 1, 0))
            upd_ref[at, :] = tail_ref[at, :] - product
            at = slice(NB * part, NB * part + NB + (8 if part == 3 else 0))
            moves.append(pltpu.make_async_copy(upd_ref.at[at, :], upd_out.at[at, :], sems.at[2 + part]))
            moves[-1].start()
        for move in moves:
            move.wait()
    store.wait()


def factor(level_no, last, offset, size_rows, row_total, pos, t, tail, factors):
    args = [pos, t, in_hbm(tail)] + ([in_hbm(factors)] if level_no else [])
    return pl.pallas_call(
        functools.partial(fac_kernel, level_no, last, offset, size_rows),
        out_shape=[
            pltpu.HBM((row_total, SEP), F32),
            jax.ShapeDtypeStruct((8, NB), F32) if last else pltpu.HBM((BND + 8, BND), F32),
        ],
        in_specs=[SMEM_SPEC, VMEM_SPEC] + [HBM_SPEC] * (len(args) - 2),
        out_specs=[HBM_SPEC, VMEM_SPEC if last else HBM_SPEC],
        scratch_shapes=[
            pltpu.VMEM((SEP, WIDE), F32),
            pltpu.VMEM((NB, NB), F32),
            pltpu.VMEM((NB, NB), F32),
            pltpu.VMEM((NB, SEP), F32),
            pltpu.VMEM((size_rows, SEP), F32),
            pltpu.VMEM((BND + 8, BND), F32),
            pltpu.VMEM((BND + 8, BND), F32),
            pltpu.SemaphoreType.DMA((6,)),
        ],
        input_output_aliases={3: 0} if level_no else {},
        compiler_params=pltpu.CompilerParams(vmem_limit_bytes=VMEM_LIMIT),
    )(*args)


def mirrored(square):
    rows = lax.broadcasted_iota(jnp.int32, square.shape, 0)
    cols = lax.broadcasted_iota(jnp.int32, square.shape, 1)
    return jnp.where(rows >= cols, square, square.T)


def remote(src, dst, send_sem, recv_sem, where):
    return pltpu.make_async_remote_copy(
        src_ref=src, dst_ref=dst, send_sem=send_sem, recv_sem=recv_sem, device_id=where, device_id_type=MESH
    )


def ring_of(count):
    me = lax.axis_index("front")
    chips = count // 2
    chip, core = me // 2, lax.rem(me, 2)
    step = 1 - 2 * core

    def place(offset):
        return lax.rem(chip + offset * step + 2 * chips, chips) * 2 + core

    def twin_of(index):
        return index + 1 - 2 * core

    return me, place, twin_of


def greet(targets):
    barrier = pltpu.get_barrier_semaphore()
    for target in targets:
        pl.semaphore_signal(barrier, inc=1, device_id=target, device_id_type=MESH)
    pl.semaphore_wait(barrier, len(targets))


CUTS = 4
TWIN_SLOT = (1, 0, 2)


def coupling_rows(me, leaf, count, levels, cols_ref, vals_ref, diag_ref, dense_ref, deep_ref):
    sub = lax.broadcasted_iota(jnp.int32, (8, WIDE), 0)
    lane = lax.broadcasted_iota(jnp.int32, (8, WIDE), 1)

    def expand(cols, vals, diag, first_id):
        sums = jnp.where(lane == sub + first_id, jnp.broadcast_to(diag, (8, WIDE)), 0.0)
        for k in range(NB):
            col = jnp.broadcast_to(cols[:, k : k + 1], (8, WIDE))
            val = jnp.broadcast_to(vals[:, k : k + 1], (8, WIDE))
            sums = sums + jnp.where(col == lane, val, 0.0)
        return sums

    def first_row(level_no, local):
        size_rows = WIDE // (count << level_no)
        return (lax.rem(leaf, 1 << level_no) * count + me) * size_rows + local

    rows = cols_ref.shape[0]

    @pl.loop(0, rows // 8)
    def group(g):
        at = pl.ds(pl.multiple_of(g * 8, 8), 8)
        first_id = first_row(1, g * 8)
        for level_no in range(2, levels):
            begin = WIDE // count - 2 * (WIDE // (count << level_no))
            first_id = jnp.where(g * 8 >= begin, first_row(level_no, g * 8 - begin), first_id)
        dense_ref[at, :] = expand(cols_ref[at, :], vals_ref[at, :], diag_ref[at, :], first_id)

    odd = rows % 8
    if odd:
        def tail_of(ref):
            part = ref[rows - odd : rows, :]
            return jnp.concatenate([part] * (8 // odd), axis=0)

        sums = expand(tail_of(cols_ref), tail_of(vals_ref), tail_of(diag_ref), first_row(levels - 1, 0))
        deep_ref[...] = jnp.concatenate([sums[:odd, :SEP], sums[:odd, SEP:]], axis=0)


def level_rows(count, level_no):
    size_rows = WIDE // (count << level_no)
    return size_rows, WIDE // count - 2 * size_rows


def leaf_copies(leaf, count, level_no, dense_ref, deep_ref, pack_ref, deep_land, sems, sending, act):
    span = 1 << level_no
    size_rows, begin = level_rows(count, level_no)
    own = lax.rem(leaf, span)

    @pl.loop(1, span)
    def step(d):
        a = own if sending else lax.rem(own - d + span, span)
        where = {"leaf": leaf - own + (lax.rem(own + d, span) if sending else own)}
        if size_rows % 8:
            act(remote(deep_ref, deep_land.at[a], sems.at[0, 0, d], sems.at[1, 0, d], where))
            return
        left = pl.ds(pl.multiple_of(a * size_rows, size_rows), size_rows)
        src = dense_ref.at[begin : begin + size_rows, :SEP]
        act(remote(src, pack_ref.at[left, :], sems.at[0, 0, d], sems.at[1, 0, d], where))

        @pl.when(a >= span // 2)
        def right_part():
            right = pl.ds(pl.multiple_of(a * size_rows + SEP // count, size_rows), size_rows)
            src = dense_ref.at[begin : begin + size_rows, SEP:]
            act(remote(src, pack_ref.at[right, :], sems.at[0, 1, d], sems.at[1, 1, d], where))


def own_copies(leaf, count, level_no, dense_ref, deep_ref, pack_ref, deep_land, sems, act):
    span = 1 << level_no
    size_rows, begin = level_rows(count, level_no)
    own = lax.rem(leaf, span)
    if size_rows % 8:
        act(pltpu.make_async_copy(deep_ref, deep_land.at[own], sems.at[0, 0, 0]))
        return
    left = pl.ds(pl.multiple_of(own * size_rows, size_rows), size_rows)
    act(pltpu.make_async_copy(dense_ref.at[begin : begin + size_rows, :SEP], pack_ref.at[left, :], sems.at[0, 0, 0]))

    @pl.when(own >= span // 2)
    def right_part():
        right = pl.ds(pl.multiple_of(own * size_rows + SEP // count, size_rows), size_rows)
        src = dense_ref.at[begin : begin + size_rows, SEP:]
        act(pltpu.make_async_copy(src, pack_ref.at[right, :], sems.at[0, 1, 0]))


def start(copy):
    copy.start()


def gather_kernel(
    count, levels, hosted, strip_in, cols_in, vals_in, diag_ref, t_ref, tail_out, *refs
):
    packs = refs[:hosted]
    (
        dense_out, deep_out, land_ref, dense_ref, deep_ref, tail_ref, strip_ref, cols_ref, vals_ref,
        send_sem, recv_sem, out_sem, *leaf_sems,
    ) = refs[hosted:]
    fetches = [
        pltpu.make_async_copy(strip_in, strip_ref, out_sem.at[3]),
        pltpu.make_async_copy(cols_in, cols_ref, out_sem.at[4]),
        pltpu.make_async_copy(vals_in, vals_ref, out_sem.at[5]),
    ]
    for copy in fetches:
        copy.start()
    leaf = lax.axis_index("leaf")
    me, place, twin_of = ring_of(count)
    rows = strip_ref.shape[0]
    cut = WIDE // CUTS
    ahead, behind, twin = {"front": place(1)}, {"front": place(-1)}, {"front": twin_of(me)}
    span = 1 << hosted
    others = [{"leaf": leaf - lax.rem(leaf, span) + lax.rem(leaf + d, span)} for d in range(1, span)]
    greet([ahead, behind, twin] + others)
    fetches[0].wait()

    def needed(index, c):
        return index * rows // cut >= c

    def move(slot, index, c, where):
        at = land_ref.at[pl.ds(pl.multiple_of(index * rows, rows), rows), cut * c : cut * c + cut]
        src = strip_ref.at[:, cut * c : cut * c + cut] if slot in (0, 1, 3) else at
        return remote(src, at, send_sem.at[slot, c], recv_sem.at[slot, c], where)

    def each(index, act):
        for c in range(CUTS):
            if c == 0:
                act(c)
            else:
                pl.when(needed(index, c))(functools.partial(act, c))

    each(me, lambda c: move(0, me, c, ahead).start())
    each(me, lambda c: move(1, me, c, behind).start())
    each(me, lambda c: move(3, me, c, twin).start())
    land_ref[pl.ds(pl.multiple_of(me * rows, rows), rows), :] = strip_ref[...]
    for copy in fetches[1:]:
        copy.wait()
    coupling_rows(me, leaf, count, levels, cols_ref, vals_ref, diag_ref, dense_ref, deep_ref)
    parts = [(leaf, count, n + 1, dense_ref, deep_ref, packs[n], None, leaf_sems[n]) for n in range(hosted)]
    for part in parts:
        leaf_copies(*part, True, start)
        own_copies(*part, start)
    outs = [
        pltpu.make_async_copy(dense_ref, dense_out, out_sem.at[0]),
        pltpu.make_async_copy(deep_ref, deep_out, out_sem.at[1]),
    ]
    for copy in outs:
        copy.start()
    sources = [place(-1), place(1), place(-2)]

    def arrive(c, k):
        index = sources[k]
        move(k, index, c, ahead).wait_recv()
        if k == 0:
            move(2, index, c, ahead).start()
        move(4 + TWIN_SLOT[k], index, c, twin).start()

    for k in range(3):
        each(sources[k], functools.partial(arrive, k=k))
    for k, index in enumerate([me] + sources):
        each(twin_of(index), lambda c: move(3 + k, twin_of(index), c, twin).wait_recv())
    tail_ref[:BND, :] = mirrored(land_ref[SEP:, SEP:])
    tail_ref[BND:, :] = jnp.zeros((8, BND), F32)
    outs.append(pltpu.make_async_copy(tail_ref, tail_out, out_sem.at[2]))
    outs[-1].start()
    t_ref[:, :SEP] = mirrored(land_ref[:SEP, :SEP])
    t_ref[:, SEP:] = land_ref[SEP:, :SEP].T
    each(me, lambda c: move(3, me, c, twin).wait_send())
    for k, index in enumerate(sources):
        each(index, lambda c: move(4 + TWIN_SLOT[k], index, c, twin).wait_send())
    each(me, lambda c: move(0, me, c, ahead).wait_send())
    each(me, lambda c: move(1, me, c, behind).wait_send())
    each(sources[0], lambda c: move(2, sources[0], c, ahead).wait_send())
    for part in parts:
        leaf_copies(*part, False, lambda copy: copy.wait_recv())
        leaf_copies(*part, True, lambda copy: copy.wait_send())
        own_copies(*part, lambda copy: copy.wait())
    for copy in outs:
        copy.wait()


def gather_front(strip, cols, vals, diag, count, leaves, cid):
    levels = leaves.bit_length()
    hosted = min(2, levels - 1)
    return pl.pallas_call(
        functools.partial(gather_kernel, count, levels, hosted),
        out_shape=[
            jax.ShapeDtypeStruct((SEP, WIDE), F32),
            pltpu.HBM((BND + 8, BND), F32),
            *[pltpu.HBM((3 * SEP // count, SEP), F32)] * hosted,
            pltpu.HBM((WIDE // count, WIDE), F32),
            pltpu.HBM((8, SEP), F32),
        ],
        in_specs=[HBM_SPEC] * 3 + [VMEM_SPEC],
        out_specs=[VMEM_SPEC] + [HBM_SPEC] * (3 + hosted),
        scratch_shapes=[
            pltpu.VMEM((WIDE, WIDE), F32),
            pltpu.VMEM((WIDE // count, WIDE), F32),
            pltpu.VMEM((8, SEP), F32),
            pltpu.VMEM((BND + 8, BND), F32),
            pltpu.VMEM(strip.shape, F32),
            pltpu.VMEM(cols.shape, jnp.int32),
            pltpu.VMEM(vals.shape, F32),
            pltpu.SemaphoreType.DMA((7, CUTS)),
            pltpu.SemaphoreType.DMA((7, CUTS)),
            pltpu.SemaphoreType.DMA((6,)),
        ]
        + [pltpu.SemaphoreType.DMA((2, 2, 2 << n)) for n in range(hosted)],
        compiler_params=pltpu.CompilerParams(
            collective_id=cid, has_side_effects=True, vmem_limit_bytes=VMEM_LIMIT
        ),
    )(in_hbm(strip), in_hbm(cols), in_hbm(vals), diag)


PART = 32


def chunk_place(index, j):
    first = index // 4 + 1
    if isinstance(index, int):
        return (index, j) if j < first else (15 - index, j - first)
    return jnp.where(j < first, index, 15 - index), jnp.where(j < first, j, j - first)


def pick_of(maps_ref, row):
    ids = lax.broadcasted_iota(jnp.int32, (WIDE, BND), 0)
    return jnp.where(ids == maps_ref[pl.ds(row, 1), :], 1.0, 0.0).astype(BF16)


def swap_kernel(count, bit, map_base, hosts, upd_in, maps_ref, low_in, *refs):
    dense_ref = deep_ref = pack_out = deep_land = None
    if hosts:
        dense_ref, deep_ref, t_ref, tail_out, pack_out, *refs = refs
    else:
        t_ref, tail_out, *refs = refs
    (
        pack_ref, land_ref, sib_ref, nat_ref, natail_ref, ct_ref, ctail_ref, slog_ref, low_ref, tlow_ref,
        upd_ref, tail_ref, log_sem, low_sem, send_sem, recv_sem, *refs,
    ) = refs
    host_level = bit + 3
    span = 1 << host_level if hosts else 2
    odd = hosts and level_rows(count, host_level)[0] % 8 != 0
    fetch = pltpu.make_async_copy(upd_in, upd_ref, low_sem.at[3])
    fetch.start()
    leaf = lax.axis_index("leaf")
    side = lax.rem(leaf // (1 << bit), 2)
    other = {"leaf": leaf + (1 - 2 * side) * (1 << bit)}
    me, place, twin_of = ring_of(count)
    ahead, behind, twin = {"front": place(1)}, {"front": place(-1)}, {"front": twin_of(me)}
    barrier = pltpu.get_barrier_semaphore()
    for target in [ahead, behind, twin] + ([] if hosts else [other]):
        pl.semaphore_signal(barrier, inc=1, device_id=target, device_id_type=MESH)
    if hosts:
        @pl.loop(1, span)
        def greet_leaf(d):
            own = lax.rem(leaf, span)
            where = {"leaf": leaf - own + lax.rem(own + d, span)}
            pl.semaphore_signal(barrier, inc=1, device_id=where, device_id_type=MESH)

        host_sem = refs[0]
        if odd:
            deep_land, gathered_ref = refs[1:]
        parts = (leaf, count, host_level, dense_ref, deep_ref, pack_out, deep_land, host_sem)
        own_copies(*parts, start)
    fetch.wait()
    for j in range(5):
        rb, cb = chunk_place(me, j)
        pack_ref[PART * j : PART * j + PART, :] = upd_ref[
            pl.ds(pl.multiple_of(rb * PART, PART), PART), pl.ds(pl.multiple_of(cb * NB, NB), NB)
        ]
    pl.semaphore_wait(barrier, 3 + span - 1)

    def move(slot, index, where):
        src = pack_ref if slot == 0 else land_ref.at[index]
        return remote(src, land_ref.at[index], send_sem.at[slot], recv_sem.at[slot], where)

    cross = move(0, me, other)
    cross.start()
    logs = remote(upd_ref.at[BND:, :NB], slog_ref, log_sem.at[0], log_sem.at[1], other)
    logs.start()

    twin_low = remote(low_in, tlow_ref, low_sem.at[0], low_sem.at[1], twin)
    twin_low.start()
    own_low = pltpu.make_async_copy(low_in, low_ref, low_sem.at[2])
    own_low.start()
    if hosts:
        leaf_copies(*parts, True, start)
    own_row = map_base + leaf // (1 << bit)
    pick = pick_of(maps_ref, own_row)
    cross.wait_recv()
    sends = [move(1, me, ahead), move(2, me, behind), move(4, me, twin)]
    for copy in sends:
        copy.start()

    uh, ul = split2(upd_ref[:BND, :])
    xh = dg(pick, uh, 1, 0).astype(BF16)
    xl = dg(pick, ul, 1, 0).astype(BF16)
    sources = [place(-1), place(1), place(-2)]
    for k in range(2):
        move(1 + k, sources[k], ahead).wait_recv()
        if k == 0:
            sends.append(move(3, sources[0], ahead))
            sends[-1].start()
        sends.append(move(5 + TWIN_SLOT[k], sources[k], twin))
        sends[-1].start()
    t_ref[...] = dg(xh[:SEP], pick, 1, 1) + dg(xl[:SEP], pick, 1, 1)
    move(3, sources[2], ahead).wait_recv()
    sends.append(move(7, sources[2], twin))
    sends[-1].start()
    tail_ref[:BND, :] = dg(xh[SEP:], pick[SEP:], 1, 1) + dg(xl[SEP:], pick[SEP:], 1, 1)
    own_low.wait()
    twin_low.wait_recv()
    size_rows = WIDE // (count << bit + 1)
    core = lax.rem(me, 2)
    for f in range(count):
        for a in range(2 << bit):
            src, dst = a * size_rows, (a * count + f) * size_rows
            mine = low_ref[f // 2, src : src + size_rows, :]
            other_rows = tlow_ref[f // 2, src : src + size_rows, :]
            nat_ref[dst : dst + size_rows, :] = jnp.where(core == f % 2, mine, other_rows)
            if dst >= SEP:
                src = SEP // count + src
                mine = low_ref[f // 2, src : src + size_rows, :]
                other_rows = tlow_ref[f // 2, src : src + size_rows, :]
                natail_ref[dst - SEP : dst - SEP + size_rows, :] = jnp.where(core == f % 2, mine, other_rows)
    ct_ref[:, :SEP] = mirrored(nat_ref[:SEP, :])
    ct_ref[:, SEP:] = nat_ref[SEP:, :].T
    ctail_ref[...] = mirrored(natail_ref[...])
    pick = pick_of(maps_ref, own_row + 1 - 2 * side)
    logs.wait_recv()
    tail_ref[BND:, :NB] = upd_ref[BND:, :NB] + slog_ref[...]
    for k, index in enumerate([me] + sources):
        move(4 + k, twin_of(index), twin).wait_recv()
    for copy in [cross, logs, twin_low] + sends:
        copy.wait_send()

    for f in range(count):
        for j in range(5):
            rb, cb = chunk_place(f, j)
            sib_ref[rb * PART : rb * PART + PART, cb * NB : cb * NB + NB] = land_ref[f, PART * j : PART * j + PART, :]
    for rb in range(BND // NB):
        for cb in range(rb):
            sib_ref[cb * NB : cb * NB + NB, rb * NB : rb * NB + NB] = sib_ref[
                rb * NB : rb * NB + NB, cb * NB : cb * NB + NB
            ].T
    uh, ul = split2(sib_ref[...])
    xh = dg(pick, uh, 1, 0).astype(BF16)
    xl = dg(pick, ul, 1, 0).astype(BF16)
    tail_ref[:BND, :] = (
        tail_ref[:BND, :] + (dg(xh[SEP:], pick[SEP:], 1, 1) + dg(xl[SEP:], pick[SEP:], 1, 1))
    ) + ctail_ref[...]
    tail_move = pltpu.make_async_copy(tail_ref, tail_out, low_sem.at[4])
    tail_move.start()
    t_ref[...] = (t_ref[...] + (dg(xh[:SEP], pick, 1, 1) + dg(xl[:SEP], pick, 1, 1))) + ct_ref[...]
    if hosts:
        leaf_copies(*parts, False, lambda copy: copy.wait_recv())
        own_copies(*parts, lambda copy: copy.wait())
        if odd:
            size_rows, _ = level_rows(count, host_level)
            for a in range(span):
                gathered_ref[a * size_rows : (a + 1) * size_rows, :] = deep_land[a, :size_rows, :]
                if a >= span // 2:
                    first = SEP // count + a * size_rows
                    gathered_ref[first : first + size_rows, :] = deep_land[a, size_rows : 2 * size_rows, :]
            pack_move = pltpu.make_async_copy(gathered_ref, pack_out, low_sem.at[5])
            pack_move.start()
            pack_move.wait()
        leaf_copies(*parts, True, lambda copy: copy.wait_send())
    tail_move.wait()


def swap_assemble(upd, maps, low, dense, deep, count, bit, map_base, levels, cid):
    hosts = bit + 3 < levels
    args = [in_hbm(upd), maps, in_hbm(low)] + ([in_hbm(dense), in_hbm(deep)] if hosts else [])
    pack_shape = (3 * SEP // count, SEP)
    outs = [jax.ShapeDtypeStruct((SEP, WIDE), F32), pltpu.HBM((BND + 8, BND), F32)]
    scratch = [
        pltpu.VMEM((5 * PART, NB), F32),
        pltpu.VMEM((count, 5 * PART, NB), F32),
        pltpu.VMEM((BND, BND), F32),
        pltpu.VMEM((WIDE, SEP), F32),
        pltpu.VMEM((BND, BND), F32),
        pltpu.VMEM((SEP, WIDE), F32),
        pltpu.VMEM((BND, BND), F32),
        pltpu.VMEM((8, NB), F32),
        pltpu.VMEM((count // 2,) + pack_shape, F32),
        pltpu.VMEM((count // 2,) + pack_shape, F32),
        pltpu.VMEM((BND + 8, BND), F32),
        pltpu.VMEM((BND + 8, BND), F32),
        pltpu.SemaphoreType.DMA((2,)),
        pltpu.SemaphoreType.DMA((6,)),
        pltpu.SemaphoreType.DMA((8,)),
        pltpu.SemaphoreType.DMA((8,)),
    ]
    if hosts:
        span = 8 << bit
        scratch.append(pltpu.SemaphoreType.DMA((2, 2, span)))
        if level_rows(count, bit + 3)[0] % 8:
            scratch += [pltpu.VMEM((span, 8, SEP), F32), pltpu.VMEM(pack_shape, F32)]
    return pl.pallas_call(
        functools.partial(swap_kernel, count, bit, map_base, hosts),
        out_shape=outs + ([pltpu.HBM(pack_shape, F32)] if hosts else []),
        in_specs=[HBM_SPEC, VMEM_SPEC, HBM_SPEC] + [HBM_SPEC] * (len(args) - 3),
        out_specs=[VMEM_SPEC, HBM_SPEC] + [HBM_SPEC] * hosts,
        scratch_shapes=scratch,
        compiler_params=pltpu.CompilerParams(
            collective_id=cid, has_side_effects=True, vmem_limit_bytes=VMEM_LIMIT
        ),
    )(*args)


def body(leaf_fronts, coupling_cols, coupling_vals, sep_diag, child_maps):
    group_count = lax.axis_size("leaf")
    front_count = lax.axis_size("front")
    level_total = group_count.bit_length()
    leaf_pos = lax.axis_index("leaf")
    front_pos = lax.axis_index("front")
    sizes = [WIDE // (front_count << level_no) for level_no in range(level_total)]
    pos = jnp.stack(
        [((leaf_pos & (1 << n) - 1) * front_count + front_pos) * sizes[n] for n in range(level_total)]
    ).astype(jnp.int32)
    same_core = [list(range(core, front_count, 2)) for core in range(2)]
    t, tail, *packs, dense, deep = gather_front(
        leaf_fronts[0], coupling_cols[0, 0], coupling_vals[0, 0], sep_diag[0, 0][:, None], front_count, group_count, 0
    )
    factors = None
    map_base = 0
    offset = 0
    for level_no in range(level_total):
        last = level_no + 1 == level_total
        if not last:
            low = lax.all_gather(packs[level_no], "front", axis=0, axis_index_groups=same_core)
        factors, upd = factor(level_no, last, offset, sizes[level_no], sum(sizes), pos, t, tail, factors)
        offset += sizes[level_no]
        if last:
            break
        t, tail, *more = swap_assemble(
            upd, child_maps, low, dense, deep, front_count, level_no, map_base, level_total, 1 + level_no
        )
        packs += more
        map_base += group_count >> level_no
    return (factors[None, None], jnp.sum(upd))


def solution(mesh):
    placed = (
        P("leaf", "front", None),
        P("leaf", "front", None, None),
        P("leaf", "front", None, None),
        P("leaf", "front", None),
        P(),
    )
    return jax.shard_map(
        body,
        mesh=mesh,
        in_specs=placed,
        out_specs=(P("leaf", "front", None, None), P()),
        check_vma=False,
    )
```

```python
import functools

import jax
import jax.numpy as jnp
from jax import lax
from jax.experimental import pallas as pl
from jax.experimental.pallas import tpu as pltpu
from jax.sharding import PartitionSpec as P

SEP = 512
BND = 512
WIDE = SEP + BND
NB = 128
F32 = jnp.float32
BF16 = jnp.bfloat16
MESH = pl.DeviceIdType.MESH
VMEM_SPEC = pl.BlockSpec(memory_space=pltpu.VMEM)
SMEM_SPEC = pl.BlockSpec(memory_space=pltpu.SMEM)
HBM_SPEC = pl.BlockSpec(memory_space=pltpu.HBM)
VMEM_LIMIT = 28 * 2**20


def in_hbm(array):
    return pltpu.with_memory_space_constraint(array, pltpu.HBM)


def split2(a):
    hi = a.astype(BF16)
    lo = (a - hi.astype(F32)).astype(BF16)
    return hi, lo


def dg(a, b, ca, cb):
    return lax.dot_general(a, b, (((ca,), (cb,)), ((), ())), preferred_element_type=F32)


def dot3(a, b):
    ah, al = split2(a)
    bh, bl = split2(b)
    return dg(ah, bh, 1, 0) + (dg(ah, bl, 1, 0) + dg(al, bh, 1, 0))


def row_of(x, j):
    return jnp.broadcast_to(x[j : j + 1, :], (8, NB))


def col_of(x, k):
    return jnp.broadcast_to(x[:, k : k + 1], (8, NB))


def diag_factor(dref, nref):
    sub = lax.broadcasted_iota(jnp.int32, (8, NB), 0)
    lane = lax.broadcasted_iota(jnp.int32, (8, NB), 1)
    zero = jnp.zeros((8, NB), F32)
    D = [dref[8 * v : 8 * v + 8, :] for v in range(16)]
    for b in range(16):
        cols = ahead if b else [col_of(D[0], k) for k in range(8)]
        if b < 15:
            ahead = [col_of(D[b + 1], 8 * b + 8 + k) for k in range(8)]
        a = {(i, k): row_of(cols[k], i) for k in range(8) for i in range(k, 8)}
        drow = [row_of(D[b], j) for j in range(8)]
        inner = (lane >= 8 * b) & (lane < 8 * b + 8)
        done = lane < 8 * b + 8
        left = jnp.where(lane < 8 * b, D[b], jnp.where(lane == sub + 8 * b, 1.0, 0.0))
        nrow = [row_of(left, j) for j in range(8)]
        r, l, u, n = {}, {}, [], []
        for j in range(8):
            r[j] = lax.rsqrt(a[j, j])
            for i in range(j + 1, 8):
                l[i, j] = a[i, j] * r[j]
            for k in range(j + 1, 8):
                for i in range(k, 8):
                    a[i, k] = a[i, k] - l[i, j] * l[k, j]
            u.append(drow[j] * r[j])
            n.append(nrow[j] * r[j])
            for i in range(j + 1, 8):
                drow[i] = drow[i] - l[i, j] * u[j]
                nrow[i] = nrow[i] - l[i, j] * n[j]
        w = [jnp.where(done, n[j], u[j]) for j in range(8)]
        for v in range(b + 1, 16):
            c = [col_of(D[v], 8 * b + k) for k in range(8)]
            dv = jnp.where(inner, 0.0, D[v])
            for j in range(8):
                lj = c[j] * r[j]
                for k in range(j + 1, 8):
                    c[k] = c[k] - lj * l[k, j]
                if v == b + 1:
                    ahead = [ahead[k] - lj * row_of(lj, k) for k in range(8)]
                dv = dv - lj * w[j]
            D[v] = dv
        db, nb = u[0], n[0]
        for j in range(1, 8):
            db = jnp.where(sub == j, u[j], db)
            nb = jnp.where(sub == j, n[j], nb)
        dref[8 * b : 8 * b + 8, :] = jnp.where(lane >= 8 * b + sub, db, zero)
        nref[8 * b : 8 * b + 8, :] = nb


def fac_kernel(level_no, last, offset, size_rows, pos_ref, t_ref, tail_in, *refs):
    if level_no:
        refs = refs[1:]
    out_ref, upd_out, u_ref, d_ref, n_ref, p_ref, piece_ref, tail_ref, upd_ref, sems = refs
    fetch = pltpu.make_async_copy(tail_in, tail_ref, sems.at[0])
    fetch.start()
    u_ref[...] = t_ref[...]
    rows = lax.broadcasted_iota(jnp.int32, (NB, NB), 0)
    cols = lax.broadcasted_iota(jnp.int32, (NB, NB), 1)
    wide = lax.broadcasted_iota(jnp.int32, (NB, WIDE), 1)

    def block(blk, logs):
        o = pl.multiple_of(blk * NB, NB)
        d_ref[...] = u_ref[pl.ds(o, NB), pl.ds(o, NB)]
        diag_factor(d_ref, n_ref)
        d = d_ref[...]
        logs = logs + jnp.sum(jnp.where(rows == cols, jnp.log(d), 0.0).reshape(16, 8, NB), axis=0)
        strip = dot3(n_ref[...], u_ref[pl.ds(o, NB), :])
        strip = jnp.where(wide >= o + NB, strip, 0.0)
        u_ref[pl.ds(o, NB), :] = strip
        u_ref[pl.ds(o, NB), pl.ds(o, NB)] = d
        sh, sl = split2(strip)

        @pl.loop(blk + 1, SEP // NB)
        def trail(jb):
            q = pl.multiple_of(jb * NB, NB)
            lh, ll = split2(u_ref[pl.ds(o, NB), pl.ds(q, NB)].T)
            u_ref[pl.ds(q, NB), :] -= dg(lh, sh, 1, 0) + (dg(lh, sl, 1, 0) + dg(ll, sh, 1, 0))

        return logs

    logs = lax.fori_loop(0, SEP // NB, block, jnp.zeros((8, NB), F32))
    start = pos_ref[level_no]
    base = pl.multiple_of(start // NB * NB, NB)
    p_ref[...] = u_ref[:, pl.ds(base, NB)].T
    if size_rows % 8 == 0:
        piece_ref[...] = p_ref[pl.ds(pl.multiple_of(start - base, 8), size_rows), :]
    else:
        part = start % 8
        block8 = p_ref[pl.ds(pl.multiple_of(start - base - part, 8), 8), :]
        picked = block8[:size_rows]
        for first in range(size_rows, 8, size_rows):
            picked = jnp.where(part == first, block8[first : first + size_rows], picked)
        piece_ref[...] = picked
    store = pltpu.make_async_copy(piece_ref, out_ref.at[offset : offset + size_rows, :], sems.at[1])
    store.start()
    fetch.wait()
    if last:
        upd_out[...] = tail_ref[BND:, :NB] + 2.0 * logs
    else:
        upd_ref[BND:, :NB] = tail_ref[BND:, :NB] + 2.0 * logs
        below = u_ref[:, SEP:]
        bh, bl = split2(below)
        th, tl = split2(below.T)
        moves = []
        for part in range(4):
            at = slice(NB * part, NB * part + NB)
            product = dg(th[at], bh, 1, 0) + (dg(th[at], bl, 1, 0) + dg(tl[at], bh, 1, 0))
            upd_ref[at, :] = tail_ref[at, :] - product
            at = slice(NB * part, NB * part + NB + (8 if part == 3 else 0))
            moves.append(pltpu.make_async_copy(upd_ref.at[at, :], upd_out.at[at, :], sems.at[2 + part]))
            moves[-1].start()
        for move in moves:
            move.wait()
    store.wait()


def factor(level_no, last, offset, size_rows, row_total, pos, t, tail, factors):
    args = [pos, t, in_hbm(tail)] + ([in_hbm(factors)] if level_no else [])
    return pl.pallas_call(
        functools.partial(fac_kernel, level_no, last, offset, size_rows),
        out_shape=[
            pltpu.HBM((row_total, SEP), F32),
            jax.ShapeDtypeStruct((8, NB), F32) if last else pltpu.HBM((BND + 8, BND), F32),
        ],
        in_specs=[SMEM_SPEC, VMEM_SPEC] + [HBM_SPEC] * (len(args) - 2),
        out_specs=[HBM_SPEC, VMEM_SPEC if last else HBM_SPEC],
        scratch_shapes=[
            pltpu.VMEM((SEP, WIDE), F32),
            pltpu.VMEM((NB, NB), F32),
            pltpu.VMEM((NB, NB), F32),
            pltpu.VMEM((NB, SEP), F32),
            pltpu.VMEM((size_rows, SEP), F32),
            pltpu.VMEM((BND + 8, BND), F32),
            pltpu.VMEM((BND + 8, BND), F32),
            pltpu.SemaphoreType.DMA((6,)),
        ],
        input_output_aliases={3: 0} if level_no else {},
        compiler_params=pltpu.CompilerParams(vmem_limit_bytes=VMEM_LIMIT),
    )(*args)


def mirrored(square):
    rows = lax.broadcasted_iota(jnp.int32, square.shape, 0)
    cols = lax.broadcasted_iota(jnp.int32, square.shape, 1)
    return jnp.where(rows >= cols, square, square.T)


def remote(src, dst, send_sem, recv_sem, where):
    return pltpu.make_async_remote_copy(
        src_ref=src, dst_ref=dst, send_sem=send_sem, recv_sem=recv_sem, device_id=where, device_id_type=MESH
    )


def ring_of(count):
    me = lax.axis_index("front")
    chips = count // 2
    chip, core = me // 2, lax.rem(me, 2)
    step = 1 - 2 * core

    def place(offset):
        return lax.rem(chip + offset * step + 2 * chips, chips) * 2 + core

    def twin_of(index):
        return index + 1 - 2 * core

    return me, place, twin_of


def greet(targets):
    barrier = pltpu.get_barrier_semaphore()
    for target in targets:
        pl.semaphore_signal(barrier, inc=1, device_id=target, device_id_type=MESH)
    pl.semaphore_wait(barrier, len(targets))


CUTS = 4
TWIN_SLOT = (1, 0, 2)


def coupling_rows(me, leaf, count, levels, cols_ref, vals_ref, diag_ref, dense_ref, deep_ref):
    sub = lax.broadcasted_iota(jnp.int32, (8, WIDE), 0)
    lane = lax.broadcasted_iota(jnp.int32, (8, WIDE), 1)

    def expand(cols, vals, diag, first_id):
        sums = jnp.where(lane == sub + first_id, jnp.broadcast_to(diag, (8, WIDE)), 0.0)
        for k in range(NB):
            col = jnp.broadcast_to(cols[:, k : k + 1], (8, WIDE))
            val = jnp.broadcast_to(vals[:, k : k + 1], (8, WIDE))
            sums = sums + jnp.where(col == lane, val, 0.0)
        return sums

    def first_row(level_no, local):
        size_rows = WIDE // (count << level_no)
        return (lax.rem(leaf, 1 << level_no) * count + me) * size_rows + local

    rows = cols_ref.shape[0]

    @pl.loop(0, rows // 8)
    def group(g):
        at = pl.ds(pl.multiple_of(g * 8, 8), 8)
        first_id = first_row(1, g * 8)
        for level_no in range(2, levels):
            begin = WIDE // count - 2 * (WIDE // (count << level_no))
            first_id = jnp.where(g * 8 >= begin, first_row(level_no, g * 8 - begin), first_id)
        dense_ref[at, :] = expand(cols_ref[at, :], vals_ref[at, :], diag_ref[at, :], first_id)

    odd = rows % 8
    if odd:
        def tail_of(ref):
            part = ref[rows - odd : rows, :]
            return jnp.concatenate([part] * (8 // odd), axis=0)

        sums = expand(tail_of(cols_ref), tail_of(vals_ref), tail_of(diag_ref), first_row(levels - 1, 0))
        deep_ref[...] = jnp.concatenate([sums[:odd, :SEP], sums[:odd, SEP:]], axis=0)


def level_rows(count, level_no):
    size_rows = WIDE // (count << level_no)
    return size_rows, WIDE // count - 2 * size_rows


def leaf_copies(leaf, count, level_no, dense_ref, deep_ref, pack_ref, deep_land, sems, sending, act):
    span = 1 << level_no
    size_rows, begin = level_rows(count, level_no)
    own = lax.rem(leaf, span)

    @pl.loop(1, span)
    def step(d):
        a = own if sending else lax.rem(own - d + span, span)
        where = {"leaf": leaf - own + (lax.rem(own + d, span) if sending else own)}
        if size_rows % 8:
            act(remote(deep_ref, deep_land.at[a], sems.at[0, 0, d], sems.at[1, 0, d], where))
            return
        left = pl.ds(pl.multiple_of(a * size_rows, size_rows), size_rows)
        src = dense_ref.at[begin : begin + size_rows, :SEP]
        act(remote(src, pack_ref.at[left, :], sems.at[0, 0, d], sems.at[1, 0, d], where))

        @pl.when(a >= span // 2)
        def right_part():
            right = pl.ds(pl.multiple_of(a * size_rows + SEP // count, size_rows), size_rows)
            src = dense_ref.at[begin : begin + size_rows, SEP:]
            act(remote(src, pack_ref.at[right, :], sems.at[0, 1, d], sems.at[1, 1, d], where))


def own_copies(leaf, count, level_no, dense_ref, deep_ref, pack_ref, deep_land, sems, act):
    span = 1 << level_no
    size_rows, begin = level_rows(count, level_no)
    own = lax.rem(leaf, span)
    if size_rows % 8:
        act(pltpu.make_async_copy(deep_ref, deep_land.at[own], sems.at[0, 0, 0]))
        return
    left = pl.ds(pl.multiple_of(own * size_rows, size_rows), size_rows)
    act(pltpu.make_async_copy(dense_ref.at[begin : begin + size_rows, :SEP], pack_ref.at[left, :], sems.at[0, 0, 0]))

    @pl.when(own >= span // 2)
    def right_part():
        right = pl.ds(pl.multiple_of(own * size_rows + SEP // count, size_rows), size_rows)
        src = dense_ref.at[begin : begin + size_rows, SEP:]
        act(pltpu.make_async_copy(src, pack_ref.at[right, :], sems.at[0, 1, 0]))


def start(copy):
    copy.start()


def gather_kernel(
    count, levels, hosted, strip_in, cols_ref, vals_ref, diag_ref, t_ref, tail_out, *refs
):
    packs = refs[:hosted]
    (
        dense_out, deep_out, land_ref, dense_ref, deep_ref, tail_ref, strip_ref,
        send_sem, recv_sem, out_sem, *leaf_sems,
    ) = refs[hosted:]
    fetch = pltpu.make_async_copy(strip_in, strip_ref, out_sem.at[3])
    fetch.start()
    leaf = lax.axis_index("leaf")
    me, place, twin_of = ring_of(count)
    rows = strip_ref.shape[0]
    cut = WIDE // CUTS
    ahead, behind, twin = {"front": place(1)}, {"front": place(-1)}, {"front": twin_of(me)}
    span = 1 << hosted
    others = [{"leaf": leaf - lax.rem(leaf, span) + lax.rem(leaf + d, span)} for d in range(1, span)]
    greet([ahead, behind, twin] + others)
    fetch.wait()

    def needed(index, c):
        return index * rows // cut >= c

    def move(slot, index, c, where):
        at = land_ref.at[pl.ds(pl.multiple_of(index * rows, rows), rows), cut * c : cut * c + cut]
        src = strip_ref.at[:, cut * c : cut * c + cut] if slot in (0, 1, 3) else at
        return remote(src, at, send_sem.at[slot, c], recv_sem.at[slot, c], where)

    def each(index, act):
        for c in range(CUTS):
            if c == 0:
                act(c)
            else:
                pl.when(needed(index, c))(functools.partial(act, c))

    each(me, lambda c: move(0, me, c, ahead).start())
    each(me, lambda c: move(1, me, c, behind).start())
    each(me, lambda c: move(3, me, c, twin).start())
    land_ref[pl.ds(pl.multiple_of(me * rows, rows), rows), :] = strip_ref[...]
    coupling_rows(me, leaf, count, levels, cols_ref, vals_ref, diag_ref, dense_ref, deep_ref)
    parts = [(leaf, count, n + 1, dense_ref, deep_ref, packs[n], None, leaf_sems[n]) for n in range(hosted)]
    for part in parts:
        leaf_copies(*part, True, start)
        own_copies(*part, start)
    outs = [
        pltpu.make_async_copy(dense_ref, dense_out, out_sem.at[0]),
        pltpu.make_async_copy(deep_ref, deep_out, out_sem.at[1]),
    ]
    for copy in outs:
        copy.start()
    sources = [place(-1), place(1), place(-2)]

    def arrive(c, k):
        index = sources[k]
        move(k, index, c, ahead).wait_recv()
        if k == 0:
            move(2, index, c, ahead).start()
        move(4 + TWIN_SLOT[k], index, c, twin).start()

    for k in range(3):
        each(sources[k], functools.partial(arrive, k=k))
    for k, index in enumerate([me] + sources):
        each(twin_of(index), lambda c: move(3 + k, twin_of(index), c, twin).wait_recv())
    tail_ref[:BND, :] = mirrored(land_ref[SEP:, SEP:])
    tail_ref[BND:, :] = jnp.zeros((8, BND), F32)
    outs.append(pltpu.make_async_copy(tail_ref, tail_out, out_sem.at[2]))
    outs[-1].start()
    t_ref[:, :SEP] = mirrored(land_ref[:SEP, :SEP])
    t_ref[:, SEP:] = land_ref[SEP:, :SEP].T
    each(me, lambda c: move(3, me, c, twin).wait_send())
    for k, index in enumerate(sources):
        each(index, lambda c: move(4 + TWIN_SLOT[k], index, c, twin).wait_send())
    each(me, lambda c: move(0, me, c, ahead).wait_send())
    each(me, lambda c: move(1, me, c, behind).wait_send())
    each(sources[0], lambda c: move(2, sources[0], c, ahead).wait_send())
    for part in parts:
        leaf_copies(*part, False, lambda copy: copy.wait_recv())
        leaf_copies(*part, True, lambda copy: copy.wait_send())
        own_copies(*part, lambda copy: copy.wait())
    for copy in outs:
        copy.wait()


def gather_front(strip, cols, vals, diag, count, leaves, cid):
    levels = leaves.bit_length()
    hosted = min(2, levels - 1)
    return pl.pallas_call(
        functools.partial(gather_kernel, count, levels, hosted),
        out_shape=[
            jax.ShapeDtypeStruct((SEP, WIDE), F32),
            pltpu.HBM((BND + 8, BND), F32),
            *[pltpu.HBM((3 * SEP // count, SEP), F32)] * hosted,
            pltpu.HBM((WIDE // count, WIDE), F32),
            pltpu.HBM((8, SEP), F32),
        ],
        in_specs=[HBM_SPEC] + [VMEM_SPEC] * 3,
        out_specs=[VMEM_SPEC] + [HBM_SPEC] * (3 + hosted),
        scratch_shapes=[
            pltpu.VMEM((WIDE, WIDE), F32),
            pltpu.VMEM((WIDE // count, WIDE), F32),
            pltpu.VMEM((8, SEP), F32),
            pltpu.VMEM((BND + 8, BND), F32),
            pltpu.VMEM(strip.shape, F32),
            pltpu.SemaphoreType.DMA((7, CUTS)),
            pltpu.SemaphoreType.DMA((7, CUTS)),
            pltpu.SemaphoreType.DMA((4,)),
        ]
        + [pltpu.SemaphoreType.DMA((2, 2, 2 << n)) for n in range(hosted)],
        compiler_params=pltpu.CompilerParams(
            collective_id=cid, has_side_effects=True, vmem_limit_bytes=VMEM_LIMIT
        ),
    )(in_hbm(strip), cols, vals, diag)


PART = 32


def chunk_place(index, j):
    first = index // 4 + 1
    if isinstance(index, int):
        return (index, j) if j < first else (15 - index, j - first)
    return jnp.where(j < first, index, 15 - index), jnp.where(j < first, j, j - first)


def pick_of(maps_ref, row):
    ids = lax.broadcasted_iota(jnp.int32, (WIDE, BND), 0)
    return jnp.where(ids == maps_ref[pl.ds(row, 1), :], 1.0, 0.0).astype(BF16)


def swap_kernel(count, bit, map_base, hosts, upd_in, maps_ref, low_in, *refs):
    dense_ref = deep_ref = pack_out = deep_land = None
    if hosts:
        dense_ref, deep_ref, t_ref, tail_out, pack_out, *refs = refs
    else:
        t_ref, tail_out, *refs = refs
    (
        pack_ref, land_ref, sib_ref, nat_ref, natail_ref, ct_ref, ctail_ref, slog_ref, low_ref, tlow_ref,
        upd_ref, tail_ref, log_sem, low_sem, send_sem, recv_sem, *refs,
    ) = refs
    host_level = bit + 3
    span = 1 << host_level if hosts else 2
    odd = hosts and level_rows(count, host_level)[0] % 8 != 0
    fetch = pltpu.make_async_copy(upd_in, upd_ref, low_sem.at[3])
    fetch.start()
    leaf = lax.axis_index("leaf")
    side = lax.rem(leaf // (1 << bit), 2)
    other = {"leaf": leaf + (1 - 2 * side) * (1 << bit)}
    me, place, twin_of = ring_of(count)
    ahead, behind, twin = {"front": place(1)}, {"front": place(-1)}, {"front": twin_of(me)}
    barrier = pltpu.get_barrier_semaphore()
    for target in [ahead, behind, twin] + ([] if hosts else [other]):
        pl.semaphore_signal(barrier, inc=1, device_id=target, device_id_type=MESH)
    if hosts:
        @pl.loop(1, span)
        def greet_leaf(d):
            own = lax.rem(leaf, span)
            where = {"leaf": leaf - own + lax.rem(own + d, span)}
            pl.semaphore_signal(barrier, inc=1, device_id=where, device_id_type=MESH)

        host_sem = refs[0]
        if odd:
            deep_land, gathered_ref = refs[1:]
        parts = (leaf, count, host_level, dense_ref, deep_ref, pack_out, deep_land, host_sem)
        own_copies(*parts, start)
    fetch.wait()
    for j in range(5):
        rb, cb = chunk_place(me, j)
        pack_ref[PART * j : PART * j + PART, :] = upd_ref[
            pl.ds(pl.multiple_of(rb * PART, PART), PART), pl.ds(pl.multiple_of(cb * NB, NB), NB)
        ]
    pl.semaphore_wait(barrier, 3 + span - 1)

    def move(slot, index, where):
        src = pack_ref if slot == 0 else land_ref.at[index]
        return remote(src, land_ref.at[index], send_sem.at[slot], recv_sem.at[slot], where)

    cross = move(0, me, other)
    cross.start()
    logs = remote(upd_ref.at[BND:, :NB], slog_ref, log_sem.at[0], log_sem.at[1], other)
    logs.start()

    twin_low = remote(low_in, tlow_ref, low_sem.at[0], low_sem.at[1], twin)
    twin_low.start()
    own_low = pltpu.make_async_copy(low_in, low_ref, low_sem.at[2])
    own_low.start()
    if hosts:
        leaf_copies(*parts, True, start)
    own_row = map_base + leaf // (1 << bit)
    pick = pick_of(maps_ref, own_row)
    cross.wait_recv()
    sends = [move(1, me, ahead), move(2, me, behind), move(4, me, twin)]
    for copy in sends:
        copy.start()

    uh, ul = split2(upd_ref[:BND, :])
    xh = dg(pick, uh, 1, 0).astype(BF16)
    xl = dg(pick, ul, 1, 0).astype(BF16)
    sources = [place(-1), place(1), place(-2)]
    for k in range(2):
        move(1 + k, sources[k], ahead).wait_recv()
        if k == 0:
            sends.append(move(3, sources[0], ahead))
            sends[-1].start()
        sends.append(move(5 + TWIN_SLOT[k], sources[k], twin))
        sends[-1].start()
    t_ref[...] = dg(xh[:SEP], pick, 1, 1) + dg(xl[:SEP], pick, 1, 1)
    move(3, sources[2], ahead).wait_recv()
    sends.append(move(7, sources[2], twin))
    sends[-1].start()
    tail_ref[:BND, :] = dg(xh[SEP:], pick[SEP:], 1, 1) + dg(xl[SEP:], pick[SEP:], 1, 1)
    own_low.wait()
    twin_low.wait_recv()
    size_rows = WIDE // (count << bit + 1)
    core = lax.rem(me, 2)
    for f in range(count):
        for a in range(2 << bit):
            src, dst = a * size_rows, (a * count + f) * size_rows
            mine = low_ref[f // 2, src : src + size_rows, :]
            other_rows = tlow_ref[f // 2, src : src + size_rows, :]
            nat_ref[dst : dst + size_rows, :] = jnp.where(core == f % 2, mine, other_rows)
            if dst >= SEP:
                src = SEP // count + src
                mine = low_ref[f // 2, src : src + size_rows, :]
                other_rows = tlow_ref[f // 2, src : src + size_rows, :]
                natail_ref[dst - SEP : dst - SEP + size_rows, :] = jnp.where(core == f % 2, mine, other_rows)
    ct_ref[:, :SEP] = mirrored(nat_ref[:SEP, :])
    ct_ref[:, SEP:] = nat_ref[SEP:, :].T
    ctail_ref[...] = mirrored(natail_ref[...])
    pick = pick_of(maps_ref, own_row + 1 - 2 * side)
    logs.wait_recv()
    tail_ref[BND:, :NB] = upd_ref[BND:, :NB] + slog_ref[...]
    for k, index in enumerate([me] + sources):
        move(4 + k, twin_of(index), twin).wait_recv()
    for copy in [cross, logs, twin_low] + sends:
        copy.wait_send()

    for f in range(count):
        for j in range(5):
            rb, cb = chunk_place(f, j)
            sib_ref[rb * PART : rb * PART + PART, cb * NB : cb * NB + NB] = land_ref[f, PART * j : PART * j + PART, :]
    for rb in range(BND // NB):
        for cb in range(rb):
            sib_ref[cb * NB : cb * NB + NB, rb * NB : rb * NB + NB] = sib_ref[
                rb * NB : rb * NB + NB, cb * NB : cb * NB + NB
            ].T
    uh, ul = split2(sib_ref[...])
    xh = dg(pick, uh, 1, 0).astype(BF16)
    xl = dg(pick, ul, 1, 0).astype(BF16)
    tail_ref[:BND, :] = (
        tail_ref[:BND, :] + (dg(xh[SEP:], pick[SEP:], 1, 1) + dg(xl[SEP:], pick[SEP:], 1, 1))
    ) + ctail_ref[...]
    tail_move = pltpu.make_async_copy(tail_ref, tail_out, low_sem.at[4])
    tail_move.start()
    t_ref[...] = (t_ref[...] + (dg(xh[:SEP], pick, 1, 1) + dg(xl[:SEP], pick, 1, 1))) + ct_ref[...]
    if hosts:
        leaf_copies(*parts, False, lambda copy: copy.wait_recv())
        own_copies(*parts, lambda copy: copy.wait())
        if odd:
            size_rows, _ = level_rows(count, host_level)
            for a in range(span):
                gathered_ref[a * size_rows : (a + 1) * size_rows, :] = deep_land[a, :size_rows, :]
                if a >= span // 2:
                    first = SEP // count + a * size_rows
                    gathered_ref[first : first + size_rows, :] = deep_land[a, size_rows : 2 * size_rows, :]
            pack_move = pltpu.make_async_copy(gathered_ref, pack_out, low_sem.at[5])
            pack_move.start()
            pack_move.wait()
        leaf_copies(*parts, True, lambda copy: copy.wait_send())
    tail_move.wait()


def swap_assemble(upd, maps, low, dense, deep, count, bit, map_base, levels, cid):
    hosts = bit + 3 < levels
    args = [in_hbm(upd), maps, in_hbm(low)] + ([in_hbm(dense), in_hbm(deep)] if hosts else [])
    pack_shape = (3 * SEP // count, SEP)
    outs = [jax.ShapeDtypeStruct((SEP, WIDE), F32), pltpu.HBM((BND + 8, BND), F32)]
    scratch = [
        pltpu.VMEM((5 * PART, NB), F32),
        pltpu.VMEM((count, 5 * PART, NB), F32),
        pltpu.VMEM((BND, BND), F32),
        pltpu.VMEM((WIDE, SEP), F32),
        pltpu.VMEM((BND, BND), F32),
        pltpu.VMEM((SEP, WIDE), F32),
        pltpu.VMEM((BND, BND), F32),
        pltpu.VMEM((8, NB), F32),
        pltpu.VMEM((count // 2,) + pack_shape, F32),
        pltpu.VMEM((count // 2,) + pack_shape, F32),
        pltpu.VMEM((BND + 8, BND), F32),
        pltpu.VMEM((BND + 8, BND), F32),
        pltpu.SemaphoreType.DMA((2,)),
        pltpu.SemaphoreType.DMA((6,)),
        pltpu.SemaphoreType.DMA((8,)),
        pltpu.SemaphoreType.DMA((8,)),
    ]
    if hosts:
        span = 8 << bit
        scratch.append(pltpu.SemaphoreType.DMA((2, 2, span)))
        if level_rows(count, bit + 3)[0] % 8:
            scratch += [pltpu.VMEM((span, 8, SEP), F32), pltpu.VMEM(pack_shape, F32)]
    return pl.pallas_call(
        functools.partial(swap_kernel, count, bit, map_base, hosts),
        out_shape=outs + ([pltpu.HBM(pack_shape, F32)] if hosts else []),
        in_specs=[HBM_SPEC, VMEM_SPEC, HBM_SPEC] + [HBM_SPEC] * (len(args) - 3),
        out_specs=[VMEM_SPEC, HBM_SPEC] + [HBM_SPEC] * hosts,
        scratch_shapes=scratch,
        compiler_params=pltpu.CompilerParams(
            collective_id=cid, has_side_effects=True, vmem_limit_bytes=VMEM_LIMIT
        ),
    )(*args)


def body(leaf_fronts, coupling_cols, coupling_vals, sep_diag, child_maps):
    group_count = lax.axis_size("leaf")
    front_count = lax.axis_size("front")
    level_total = group_count.bit_length()
    leaf_pos = lax.axis_index("leaf")
    front_pos = lax.axis_index("front")
    sizes = [WIDE // (front_count << level_no) for level_no in range(level_total)]
    pos = jnp.stack(
        [((leaf_pos & (1 << n) - 1) * front_count + front_pos) * sizes[n] for n in range(level_total)]
    ).astype(jnp.int32)
    same_core = [list(range(core, front_count, 2)) for core in range(2)]
    t, tail, *packs, dense, deep = gather_front(
        leaf_fronts[0], coupling_cols[0, 0], coupling_vals[0, 0], sep_diag[0, 0][:, None], front_count, group_count, 0
    )
    factors = None
    map_base = 0
    offset = 0
    for level_no in range(level_total):
        last = level_no + 1 == level_total
        if not last:
            low = lax.all_gather(packs[level_no], "front", axis=0, axis_index_groups=same_core)
        factors, upd = factor(level_no, last, offset, sizes[level_no], sum(sizes), pos, t, tail, factors)
        offset += sizes[level_no]
        if last:
            break
        t, tail, *more = swap_assemble(
            upd, child_maps, low, dense, deep, front_count, level_no, map_base, level_total, 1 + level_no
        )
        packs += more
        map_base += group_count >> level_no
    return (factors[None, None], jnp.sum(upd))


def solution(mesh):
    placed = (
        P("leaf", "front", None),
        P("leaf", "front", None, None),
        P("leaf", "front", None, None),
        P("leaf", "front", None),
        P(),
    )
    return jax.shard_map(
        body,
        mesh=mesh,
        in_specs=placed,
        out_specs=(P("leaf", "front", None, None), P()),
        check_vma=False,
    )
```
